128 devices in a mesh: dp: 16 (over z, x), mp: 8 (over y, core).
Axes of the slice: x: 4, y: 4, z: 4, core: 2. Of those that a mesh axis runs over, the one named last changes fastest.
Arguments:
- tokens: bfloat16 [32, 512, 1024], P('dp', 'mp'), may hold values from -6 to 6
- segment_ids: int32 [32, 512], P('dp'), may hold values from 0 to 9, as said below
- qkv_weight: bfloat16 [3, 1024, 1024], P(None, 'dp', 'mp'), may hold values from -0.1875 to 0.1875
- out_weight: bfloat16 [1024, 1024], P('mp', 'dp'), may hold values from -1.5 to 1.5
- up_weight: bfloat16 [1024, 4096], P('dp', 'mp'), may hold values from -0.1875 to 0.1875
- down_weight: bfloat16 [4096, 1024], P('mp', 'dp'), may hold values from -0.125 to 0.125
- head_bias: float32 [2, 1024], P(None, 'mp'), may hold values from -0.625 to 0.625
- up_bias: float32 [4096], P('mp'), may hold values from -3 to 3
- gains: float32 [2, 1024], replicated, may hold values from 0.5 to 1.5
- shifts: float32 [4, 1024], replicated, may hold values from -3 to 3
- cotangent: bfloat16 [32, 512, 1024], P('dp', 'mp'), may hold values from -6 to 6
Outputs:
- result: bfloat16 [32, 512, 1024], P('dp', 'mp')
- grad_tokens: float32 [32, 512, 1024], P('dp', 'mp')
- grad_qkv_weight: float32 [3, 1024, 1024], P(None, 'dp', 'mp')
- grad_out_weight: float32 [1024, 1024], P('mp', 'dp')
- grad_up_weight: float32 [1024, 4096], P('dp', 'mp')
- grad_down_weight: float32 [4096, 1024], P('mp', 'dp')
- grad_head_bias: float32 [2, 1024], P(None, 'mp')
- grad_up_bias: float32 [4096], P('mp')
- grad_gains: float32 [2, 1024], replicated
- grad_shifts: float32 [4, 1024], replicated
The draws below stay inside these ranges and needn't reach their ends.
Inputs may be any that keep to these rules, and one draw needn't show every extreme that they name: `segment_ids`: in each sequence the ids start at 0 and rise by one at each new document; every document has 50 to 512 tokens. Among the 2 sequences of each index of dp, one is a single document of 512 tokens and another holds 10 documents.
All inputs are finite; a program needn't handle non-finite values.
Results may differ from the reference program's by a relative error of at most 0.023.
Values may be sent and summed in bfloat16 or wider, within the bound.
No kernel may reach another device: no remote copies, remote signals or barrier semaphores. Data moves between devices by JAX's collectives and lax.ppermute only.
A program may use at most 128 MiB of HBM per device.

```python
import math
import jax
import jax.numpy as jnp
from jax import lax

D = 1024
FF = 4096
HEADS = 16
HEAD_DIM = 64
LEN = 512
MIN_DOC = 50
MICRO = 2
SEQUENCES = 32


def draw_segment_ids(key, part):
    key = jax.random.fold_in(key, 11)
    key_count, key_pick, key_other, key_cuts = jax.random.split(key, 4)
    most_docs = LEN // MIN_DOC
    groups = SEQUENCES // MICRO
    doc_counts = jax.random.randint(key_count, (SEQUENCES,), 1, most_docs + 1)
    single_pick = jax.random.randint(key_pick, (groups,), 0, MICRO)
    packed_pick = (single_pick + jax.random.randint(key_other, (groups,), 1, MICRO)) % MICRO
    local_index = jnp.arange(SEQUENCES) % MICRO
    single_rows = jnp.repeat(single_pick, MICRO)
    packed_rows = jnp.repeat(packed_pick, MICRO)
    doc_counts = jnp.where(local_index == single_rows, 1, jnp.where(local_index == packed_rows, most_docs, doc_counts))
    spare = LEN - MIN_DOC * doc_counts
    cut_points = jax.random.randint(key_cuts, (SEQUENCES, most_docs - 1), 0, spare[:, None] + 1)
    cut_points = jnp.sort(cut_points, axis=1)
    bound_index = jnp.arange(1, most_docs)
    bounds = MIN_DOC * bound_index[None, :] + cut_points
    bounds = jnp.where(bound_index[None, :] < doc_counts[:, None], bounds, LEN + 1)
    positions = jnp.arange(LEN)
    crossed = positions[None, :, None] >= bounds[:, None, :]
    return jnp.sum(crossed.astype(jnp.int32), axis=2).astype(jnp.int32)


def block_scale(key, shape, pieces, smallest, top_value):
    def one(dim, parts):
        heights = jax.random.uniform(jax.random.fold_in(jax.random.fold_in(key, 6), dim), (parts,), jnp.float32, smallest / len(pieces), top_value / len(pieces))
        return jnp.repeat(jnp.exp(heights), shape[dim] // parts).reshape((-1,) + (1,) * (len(shape) - dim - 1))

    level = one(*pieces[0])
    for cut in pieces[1:]:
        level = level * one(*cut)
    return level


def gaussian(own_key, shape, scale, reach, pieces=(), dtype=jnp.bfloat16):
    values = jax.random.normal(own_key, shape, jnp.float32) * scale
    if len(pieces) > 0:
        values = block_scale(own_key, shape, pieces, -0.22, 0.18) * values
    return jnp.clip(values, min=-reach, max=reach).astype(dtype)


def setup_inputs(seed: int = 0) -> dict:
    arg_keys = jax.random.split(jax.random.key(seed), 12)
    tokens = gaussian(arg_keys[0], (SEQUENCES, LEN, D), 1.0, 6.0, ((0, 16), (1, 8)))
    segment_ids = draw_segment_ids(jax.random.fold_in(arg_keys[11], 71), 0)
    qkv_weight = gaussian(arg_keys[2], (3, D, D), D ** -0.5, 0.1875, ((1, 16), (2, 8)))
    out_weight = gaussian(arg_keys[3], (D, D), (D // 64) ** -0.5, 1.5, ((0, 8), (1, 16)))
    up_weight = gaussian(arg_keys[4], (D, FF), D ** -0.5, 0.1875, ((0, 16), (1, 8)))
    down_weight = gaussian(arg_keys[5], (FF, D), (FF // 2) ** -0.5, 0.125, ((0, 8), (1, 16)))
    head_bias = gaussian(arg_keys[6], (2, D), 0.1, 0.625, ((1, 8),), jnp.float32)
    up_bias = gaussian(arg_keys[7], (FF,), 0.5, 3.0, ((0, 8),), jnp.float32)
    gains = jnp.clip(1.0 + 0.1 * jax.random.normal(arg_keys[8], (2, D), jnp.float32), 0.5, 1.5)
    shifts = gaussian(arg_keys[9], (4, D), 0.5, 3.0, (), jnp.float32)
    cotangent = gaussian(arg_keys[10], (SEQUENCES, LEN, D), 1.0, 6.0, ((0, 16), (1, 8)))
    return {"tokens": tokens, "segment_ids": segment_ids, "qkv_weight": qkv_weight, "out_weight": out_weight, "up_weight": up_weight, "down_weight": down_weight, "head_bias": head_bias, "up_bias": up_bias, "gains": gains, "shifts": shifts, "cotangent": cotangent}


@jax.custom_vjp
def low(v):
    return lax.optimization_barrier(v.astype(jnp.bfloat16)).astype(jnp.float32)

@jax.custom_vjp
def low_back(v):
    return v

def low_keep(v):
    return (low(v), None)

def low_pass(kept, grad):
    return (grad,)

def back_keep(v):
    return (v, None)

def back_low(kept, grad):
    return (low(grad),)
low.defvjp(low_keep, low_pass)
low_back.defvjp(back_keep, back_low)
EPSILON = 1e-12
HIGHEST = lax.Precision.HIGHEST

def layer_norm(resid):
    centered = resid - lax.optimization_barrier(jnp.mean(resid, axis=-1, keepdims=True))
    variance = lax.optimization_barrier(jnp.mean(centered * centered, axis=-1, keepdims=True))
    return centered * lax.rsqrt(variance + EPSILON)

def seq_block(params, doc_ids, inputs):
    qkv_w, out_w, up_w, down_w, head_bias, up_bias, gains, shifts = params
    group_size = inputs.shape[0]
    projected = jnp.einsum('gtd,cde->cgte', inputs, qkv_w, precision=HIGHEST)
    query_rows = low(low_back(projected[0]) + head_bias[0])
    key_rows = low(low_back(projected[1]))
    value_rows = low(low_back(projected[2]) + head_bias[1])
    head_shape = (group_size, LEN, HEADS, HEAD_DIM)
    query_heads = query_rows.reshape(head_shape)
    key_heads = key_rows.reshape(head_shape)
    value_heads = value_rows.reshape(head_shape)
    raw_scores = jnp.einsum('gqhd,gkhd->ghqk', query_heads, key_heads, precision=HIGHEST) * HEAD_DIM ** (-0.5)
    scores = low_back(raw_scores)
    same_doc = doc_ids[:, None, :, None] == doc_ids[:, None, None, :]
    masked = jnp.where(same_doc, scores, -1e+30)
    log_total = jax.nn.logsumexp(masked, axis=-1, keepdims=True)
    prob_low = low(jnp.exp(masked - log_total))
    head_out = jnp.einsum('ghqk,gkhd->gqhd', prob_low, value_heads, precision=HIGHEST).reshape(group_size, LEN, D)
    head_out = low_back(low(head_out))
    attended = low_back(jnp.einsum('gte,ed->gtd', head_out, out_w, precision=HIGHEST)) + shifts[0]
    normed = layer_norm(inputs + attended) * gains[0] + shifts[1]
    pre_up = low_back(jnp.einsum('gtd,df->gtf', low(normed), up_w, precision=HIGHEST)) + up_bias
    activated = low(jax.nn.gelu(pre_up, approximate=False))
    feedforward = low_back(jnp.einsum('gtf,fd->gtd', activated, down_w, precision=HIGHEST)) + shifts[2]
    return layer_norm(normed + feedforward) * gains[1] + shifts[3]

def reference(tokens, segment_ids, qkv_weight, out_weight, up_weight, down_weight, head_bias, up_bias, gains, shifts, cotangent):
    group_size = math.gcd(SEQUENCES, 8)
    id_blocks = segment_ids.reshape(SEQUENCES // group_size, group_size, LEN)

    def forward(tok_in, qkv_w, out_w, up_w, down_w, bias_heads, bias_units, gain_pair, shift_rows):
        params = (qkv_w, out_w, up_w, down_w, bias_heads, bias_units, gain_pair, shift_rows)
        tok_blocks = tok_in.reshape(SEQUENCES // group_size, group_size, LEN, D)

        def apply_block(piece_pair):
            return seq_block(params, piece_pair[1], piece_pair[0])
        result_blocks = lax.map(jax.checkpoint(apply_block), (tok_blocks, id_blocks))
        return result_blocks.reshape(SEQUENCES, LEN, D)
    primals = (tokens.astype(jnp.float32), qkv_weight.astype(jnp.float32), out_weight.astype(jnp.float32), up_weight.astype(jnp.float32), down_weight.astype(jnp.float32), head_bias, up_bias, gains, shifts)
    result, pullback = jax.vjp(forward, *primals)
    grads = pullback(cotangent.astype(jnp.float32))
    return (result.astype(jnp.bfloat16), grads[0], grads[1], grads[2], grads[3], grads[4], grads[5], grads[6], grads[7], grads[8])
```

```python
import jax
import jax.numpy as jnp
from jax import lax
from jax.sharding import Mesh
from jax.sharding import PartitionSpec as P

HEAD_DIM = 64
EPSILON = 1e-12
SCALE = HEAD_DIM ** (-0.5)
F32 = jnp.float32
BF16 = jnp.bfloat16
RING = 4


def shift(value, axis, step):
    return lax.ppermute(value, axis, [(i, (i + step) % RING) for i in range(RING)])


def sibling(value):
    return lax.ppermute(value, "core", [(0, 1), (1, 0)])


def gather_tokens(rows):
    mine = [rows, shift(rows, "y", -1), shift(rows, "y", 2), shift(rows, "y", 1)]
    theirs = [sibling(block) for block in mine]
    return jnp.stack([jnp.stack(mine, 1), jnp.stack(theirs, 1)], 1)


def scatter_tokens(partial):
    other = sibling(partial[:, 1])
    total = partial[:, 0].astype(F32) + other.astype(F32)
    low = total.astype(BF16)
    got = [shift(low[:, 1], "y", 1), shift(low[:, 2], "y", 2), shift(low[:, 3], "y", -1)]
    return total[:, 0] + got[0].astype(F32) + got[1].astype(F32) + got[2].astype(F32)


def scatter_axis(blocks, axis):
    here = lax.axis_index(axis)

    def block(step):
        return lax.dynamic_index_in_dim(blocks, (here + step) % RING, 0, keepdims=False)

    got = [shift(block(1), axis, 1), shift(block(2), axis, 2), shift(block(3), axis, -1)]
    return block(0).astype(F32) + got[0].astype(F32) + got[1].astype(F32) + got[2].astype(F32)


def scatter_dp(grad):
    rows, cols = grad.shape
    cut = grad.reshape(RING, RING, 2, rows // 32, cols)
    first = scatter_axis(scatter_axis(cut[:, :, 0], "z").astype(BF16), "x")
    second = scatter_axis(scatter_axis(jnp.swapaxes(cut[:, :, 1], 0, 1), "x").astype(BF16), "z")
    return jnp.concatenate([first, second], 0)


def sum_axis(value, axis):
    return (value + shift(value, axis, 2)) + (shift(value, axis, 1) + shift(value, axis, -1))


def normalise(resid):
    centered = resid - jnp.mean(resid, axis=-1, keepdims=True)
    variance = jnp.mean(centered * centered, axis=-1, keepdims=True)
    inverse = lax.rsqrt(variance + EPSILON)
    return centered * inverse, inverse


def normalise_back(cot, unit, inverse):
    return (
        cot
        - jnp.mean(cot, axis=-1, keepdims=True)
        - unit * jnp.mean(cot * unit, axis=-1, keepdims=True)
    ) * inverse


def dot(left, right, dims):
    return lax.dot_general(left, right, ((dims[0], dims[1]), ((), ())), preferred_element_type=F32)


def on_device(
    tokens,
    segment_ids,
    qkv_weight,
    out_weight,
    up_weight,
    down_weight,
    head_bias,
    up_bias,
    gains,
    shifts,
    cotangent,
):
    seqs, rows, width = tokens.shape
    length = segment_ids.shape[1]
    count = seqs * length
    head_width = qkv_weight.shape[2]
    units = up_weight.shape[1]
    heads = head_width // HEAD_DIM
    y = lax.axis_index("y")
    core = lax.axis_index("core")

    w_qkv = lax.all_gather(
        jnp.concatenate([qkv_weight[0], qkv_weight[1], qkv_weight[2]], 1),
        ("z", "x"),
        axis=0,
        tiled=True,
    )
    w_rest = lax.all_gather(
        jnp.concatenate([out_weight.T, up_weight, down_weight.T], 1), ("z", "x"), axis=0, tiled=True
    )
    w_out = w_rest[:, :head_width]
    w_up = w_rest[:, head_width : head_width + units]
    w_down = w_rest[:, head_width + units :]

    ids = segment_ids.reshape(seqs, RING, 2, rows)
    ids = jnp.concatenate([ids, ids], 1)
    ids = lax.dynamic_slice_in_dim(ids, y, RING, 1)
    ids = jnp.where(core == 0, ids, ids[:, :, ::-1])
    ids = jnp.swapaxes(ids, 1, 2).reshape(seqs, length)
    same_doc = (ids[:, :, None] == ids[:, None, :])[:, None]

    token_all = gather_tokens(tokens).reshape(count, width)
    projected = dot(token_all, w_qkv, ((1,), (0,)))
    query = (projected[:, :head_width] + head_bias[0]).astype(BF16)
    key = projected[:, head_width : 2 * head_width].astype(BF16)
    value = (projected[:, 2 * head_width :] + head_bias[1]).astype(BF16)
    head_shape = (seqs, length, heads, HEAD_DIM)
    query = query.reshape(head_shape)
    key = key.reshape(head_shape)
    value = value.reshape(head_shape)
    scores = jnp.einsum("sqhd,skhd->shqk", query, key, preferred_element_type=F32) * SCALE
    scores = jnp.where(same_doc, scores, -1e30)
    log_total = jax.nn.logsumexp(scores, axis=-1, keepdims=True)
    probs = jnp.exp(scores - log_total)
    prob_low = probs.astype(BF16)
    head_out = jnp.einsum("shqk,skhd->sqhd", prob_low, value, preferred_element_type=F32)
    head_out = head_out.reshape(count, head_width).astype(BF16)

    token_shape = (seqs, 2, RING, rows, width)
    attn_part = dot(head_out, w_out, ((1,), (1,))).astype(BF16).reshape(token_shape)
    resid1 = tokens.astype(F32) + scatter_tokens(attn_part) + shifts[0]
    unit1, inverse1 = normalise(resid1)
    normed = unit1 * gains[0] + shifts[1]
    hidden_all = gather_tokens(normed.astype(BF16)).reshape(count, width)
    pre_up = dot(hidden_all, w_up, ((1,), (0,))) + up_bias
    cdf = 0.5 * (1.0 + lax.erf(pre_up * 0.5**0.5))
    activated = (pre_up * cdf).astype(BF16)
    slope = cdf + pre_up * jnp.exp(-0.5 * pre_up * pre_up) * 0.3989422804014327
    ffn_part = dot(activated, w_down, ((1,), (1,))).astype(BF16).reshape(token_shape)
    resid2 = normed + scatter_tokens(ffn_part) + shifts[2]
    unit2, inverse2 = normalise(resid2)
    result = (unit2 * gains[1] + shifts[3]).astype(BF16)

    cot = cotangent.astype(F32)
    d_resid2 = normalise_back(cot * gains[1], unit2, inverse2)
    d_ffn_all = gather_tokens(d_resid2.astype(BF16)).reshape(count, width)
    d_activated = dot(d_ffn_all, w_down, ((1,), (0,)))
    d_pre = d_activated * slope
    d_pre_low = d_pre.astype(BF16)
    hidden_part = dot(d_pre_low, w_up, ((1,), (1,))).astype(BF16).reshape(token_shape)
    d_normed = d_resid2 + scatter_tokens(hidden_part)
    grad_up = dot(hidden_all, d_pre_low, ((0,), (0,))).astype(BF16)
    grad_down = dot(d_ffn_all, activated, ((0,), (0,))).astype(BF16)
    grad_ffn = scatter_dp(jnp.concatenate([grad_up, grad_down], 1))

    d_resid1 = normalise_back(d_normed * gains[0], unit1, inverse1)
    d_attn_all = gather_tokens(d_resid1.astype(BF16)).reshape(count, width)
    d_heads = dot(d_attn_all, w_out, ((1,), (0,))).astype(BF16)
    grad_out = dot(d_attn_all, head_out, ((0,), (0,))).astype(BF16)
    d_heads = d_heads.reshape(head_shape)
    d_prob = jnp.einsum("sqhd,skhd->shqk", d_heads, value, preferred_element_type=F32)
    row_dot = jnp.sum(probs * d_prob, axis=-1, keepdims=True)
    d_score = (probs * (d_prob - row_dot)).astype(BF16)
    d_query = jnp.einsum("shqk,skhd->sqhd", d_score, key, preferred_element_type=F32) * SCALE
    d_key = jnp.einsum("shqk,sqhd->skhd", d_score, query, preferred_element_type=F32) * SCALE
    d_value = jnp.einsum("shqk,sqhd->skhd", prob_low, d_heads, preferred_element_type=F32)
    d_query = d_query.reshape(count, head_width)
    d_value = d_value.reshape(count, head_width)
    d_proj = jnp.concatenate(
        [d_query.astype(BF16), d_key.reshape(count, head_width).astype(BF16), d_value.astype(BF16)], 1
    )
    token_part = dot(d_proj, w_qkv, ((1,), (1,))).astype(BF16).reshape(token_shape)
    grad_tokens = d_resid1 + scatter_tokens(token_part)
    grad_qkv = dot(token_all, d_proj, ((0,), (0,))).astype(BF16)
    grad_attn = scatter_dp(jnp.concatenate([grad_qkv, grad_out], 1))

    def total(terms):
        return jnp.sum(terms, axis=(0, 1))

    norm_terms = jnp.stack(
        [
            total(d_normed * unit1),
            total(cot * unit2),
            total(d_resid1),
            total(d_normed),
            total(d_resid2),
            total(cot),
        ]
    )
    norm_terms = norm_terms + sibling(norm_terms)
    norm_terms = sum_axis(norm_terms, "y")
    unit_terms = jnp.sum(d_pre, axis=0).reshape(units // width + (units % width > 0), -1)
    unit_terms = jnp.pad(unit_terms, ((0, 0), (0, width - unit_terms.shape[1])))
    small = jnp.concatenate([norm_terms, unit_terms], 0)
    small = sum_axis(sum_axis(small, "z"), "x")
    bias_terms = jnp.stack([jnp.sum(d_query, axis=0), jnp.sum(d_value, axis=0)])
    bias_terms = sum_axis(sum_axis(bias_terms, "z"), "x")

    return (
        result,
        grad_tokens,
        jnp.stack([grad_attn[:, i * head_width : (i + 1) * head_width] for i in range(3)]),
        grad_attn[:, 3 * head_width :].T,
        grad_ffn[:, :units],
        grad_ffn[:, units:].T,
        bias_terms,
        small[6, :units],
        small[:2],
        small[2:6],
    )


def solution(mesh):
    mesh = Mesh(mesh.devices.reshape(RING, RING, RING, 2), ("z", "x", "y", "core"))
    dp, mp = ("z", "x"), ("y", "core")
    in_specs = (
        P(dp, mp, None),
        P(dp, None),
        P(None, dp, mp),
        P(mp, dp),
        P(dp, mp),
        P(mp, dp),
        P(None, mp),
        P(mp),
        P(),
        P(),
        P(dp, mp, None),
    )
    out_specs = (
        P(dp, mp, None),
        P(dp, mp, None),
        P(None, dp, mp),
        P(mp, dp),
        P(dp, mp),
        P(mp, dp),
        P(None, mp),
        P(mp),
        P(),
        P(),
    )
    return jax.shard_map(
        on_device, mesh=mesh, in_specs=in_specs, out_specs=out_specs, check_vma=False
    )
```

```python
import functools

import jax
import jax.numpy as jnp
from jax import lax
from jax.experimental import pallas as pl
from jax.experimental.pallas import tpu as pltpu
from jax.sharding import Mesh
from jax.sharding import PartitionSpec as P

HEAD_DIM = 64
EPSILON = 1e-12
SCALE = HEAD_DIM ** (-0.5)
F32 = jnp.float32
BF16 = jnp.bfloat16
RING = 4
CHUNK = 256
MIB = 2**20


def shift(value, axis, step):
    return lax.ppermute(value, axis, [(i, (i + step) % RING) for i in range(RING)])


def sibling(value):
    return lax.ppermute(value, "core", [(0, 1), (1, 0)])


def assemble(blocks):
    return jnp.concatenate(blocks, 0)


def from_chips(rows):
    return [rows, shift(rows, "y", -1), shift(rows, "y", 2), shift(rows, "y", 1)]


def gather_tokens(rows):
    mine = assemble(from_chips(rows))
    return mine, sibling(mine)


def scatter_sides(mine, theirs):
    other = sibling(theirs)
    rows = mine.shape[0] // RING
    cuts = [slice(i * rows, (i + 1) * rows) for i in (1, 2, 3)]
    return [mine, other], [(mine[c].astype(F32) + other[c].astype(F32)).astype(BF16) for c in cuts]


def scatter_chips(low):
    return [shift(low[0], "y", 1), shift(low[1], "y", 2), shift(low[2], "y", -1)]


def after(value, *others):
    return lax.optimization_barrier((value, *others))[0]


def gather_direct(rows, axis):
    return [rows, shift(rows, axis, -1), shift(rows, axis, 2), shift(rows, axis, 1)]


def gather_ring(rows, axis):
    half = rows.shape[0] // 2
    one, three = shift(rows, axis, -1), shift(rows, axis, 1)
    low, high = shift(one[:half], axis, -1), shift(three[half:], axis, 1)
    return [rows, one, low, high, three]


def pack(values, rows):
    high = lax.reduce_precision(values, 8, 7)
    room = jnp.zeros((rows - 2 * values.shape[0], values.shape[1]), BF16)
    return jnp.concatenate([high.astype(BF16), (values - high).astype(BF16), room], 0)


def unpack(packed, count):
    return packed[:count].astype(F32) + packed[count : 2 * count].astype(F32)


def same_sum(terms):
    return (terms[0] + terms[2]) + (terms[1] + terms[3])


def exchange(messages, axis):
    return [
        messages[0],
        shift(messages[1], axis, 1),
        shift(messages[2], axis, 2),
        shift(messages[3], axis, -1),
    ]


def ring_first(blocks, axis):
    return shift(blocks[2], axis, 1), shift(blocks[3], axis, -1)


def ring_second(blocks, got, axis):
    low, high = got
    half = low.shape[0]
    right = (blocks[1][:half].astype(F32) + low.astype(F32)).astype(BF16)
    left = (blocks[4][half:].astype(F32) + high.astype(F32)).astype(BF16)
    right = shift(jnp.concatenate([right, blocks[1][half:]], 0), axis, 1)
    left = shift(jnp.concatenate([blocks[4][:half], left], 0), axis, -1)
    return blocks[0], right, left


def normalise(resid):
    centered = resid - jnp.mean(resid, axis=-1, keepdims=True)
    variance = jnp.mean(centered * centered, axis=-1, keepdims=True)
    inverse = lax.rsqrt(variance + EPSILON)
    return centered * inverse, inverse


def normalise_back(cot, unit, inverse):
    return (
        cot
        - jnp.mean(cot, axis=-1, keepdims=True)
        - unit * jnp.mean(cot * unit, axis=-1, keepdims=True)
    ) * inverse


def dot(left, right, dims):
    return lax.dot_general(left, right, ((dims[0], dims[1]), ((), ())), preferred_element_type=F32)


ROW, COL = ((1,), (0,)), ((1,), (1,))
DOWN = ((0,), (0,))


def cost(micros):
    return pl.CostEstimate(flops=int(micros * 1.15e9), bytes_accessed=2**20, transcendentals=0)


def call(micros, kernel, outs, grid=(), in_specs=None, out_specs=None, mib=16):
    whole = pl.BlockSpec(memory_space=pltpu.VMEM)
    return pl.pallas_call(
        kernel,
        out_shape=[jax.ShapeDtypeStruct(shape, dtype) for shape, dtype in outs],
        grid=grid,
        in_specs=in_specs,
        out_specs=out_specs or [whole] * len(outs),
        cost_estimate=cost(micros),
        compiler_params=pltpu.CompilerParams(vmem_limit_bytes=mib * MIB),
    )


def weights_kernel(qkv_ref, out_ref, up_ref, down_ref, packed_ref):
    turned = [out_ref[...].T, up_ref[...], down_ref[...].T]
    packed_ref[...] = jnp.concatenate([qkv_ref[0], qkv_ref[1], qkv_ref[2], *turned], 1)


def by_index_kernel(count, here_ref, *refs):
    blocks, outs = refs[:count], refs[count:]
    rows = blocks[0].shape[0]
    at = 0
    for ref in blocks:
        index = (here_ref[0] + at // rows) % RING
        start = pl.multiple_of(index * rows + at % rows, 16)
        at += ref.shape[0]
        left = 0
        for out_ref in outs:
            cols = out_ref.shape[1]
            out_ref[pl.ds(start, ref.shape[0]), :] = ref[:, left : left + cols]
            left += cols


def by_index(blocks, axis, cuts=None):
    rows, cols = blocks[0].shape
    vmem = pl.BlockSpec(memory_space=pltpu.VMEM)
    outs = [(RING * rows, n) for n in cuts or [cols]]
    found = pl.pallas_call(
        functools.partial(by_index_kernel, len(blocks)),
        out_shape=[jax.ShapeDtypeStruct(shape, BF16) for shape in outs],
        grid_spec=pltpu.PrefetchScalarGridSpec(
            num_scalar_prefetch=1,
            grid=(1,),
            in_specs=[vmem] * len(blocks),
            out_specs=[vmem] * len(outs),
        ),
        cost_estimate=cost(1),
        compiler_params=pltpu.CompilerParams(vmem_limit_bytes=16 * MIB),
    )(lax.axis_index(axis).astype(jnp.int32).reshape(1), *blocks)
    return found if cuts else found[0]


def head_lanes(width):
    lane = lax.broadcasted_iota(jnp.int32, (1, width), 1)
    return [(lane // HEAD_DIM) == h for h in range(width // HEAD_DIM)]


def heads_kernel(*refs):
    *blocks, out_ref = refs
    width = blocks[0].shape[1]
    count = out_ref.shape[0] // 2
    rows = count // 2 // RING
    for j, ref in enumerate(blocks):
        cols = slice(j * width, (j + 1) * width)
        out_ref[count:, cols] = ref[count:]
        for at in range(0, count, count // 2):
            cut = (RING - j) * rows
            if j:
                out_ref[at : at + j * rows, cols] = ref[at + cut : at + count // 2]
            out_ref[at + j * rows : at + count // 2, cols] = ref[at : at + cut]


def two_sides(mine_ref, theirs_ref):
    width = mine_ref.shape[-1]
    return jnp.concatenate(
        [mine_ref[...].reshape(-1, width), theirs_ref[...].reshape(-1, width)], 0
    )


def head_scores(query, key, lanes, same_doc):
    query = jnp.where(lanes, query, jnp.zeros_like(query))
    return jnp.where(same_doc, dot(query, key, COL) * SCALE, -1e30)


def attend_kernel(mine_ref, theirs_ref, w_ref, bias_ref, id_col, id_row, qkv_ref, out_ref, log_ref):
    width = out_ref.shape[-1]
    projected = dot(two_sides(mine_ref, theirs_ref), w_ref[:, : 3 * width], ROW)
    qkv = (projected + bias_ref[...]).astype(BF16)
    qkv_ref[0] = qkv
    query, key, value = (qkv[:, i * width : (i + 1) * width] for i in range(3))
    same_doc = id_col[0] == id_row[0]
    out = jnp.zeros((qkv.shape[0], width), F32)
    for h, lanes in enumerate(head_lanes(width)):
        scores = head_scores(query, key, lanes, same_doc)
        top = jnp.max(scores, axis=1, keepdims=True)
        weight = jnp.exp(scores - top)
        total = jnp.sum(weight, axis=1, keepdims=True)
        log_ref[0, :, h : h + 1] = top + jnp.log(total)
        low = (weight * (1.0 / total)).astype(BF16)
        out = jnp.where(lanes, dot(low, value, ROW), out)
    out_ref[...] = out.astype(BF16).reshape(out_ref.shape)


def attend_back_kernel(
    mine_ref, theirs_ref, w_ref, qkv_ref, log_ref, id_col, id_row,
    d_ref, bias_ref, part_mine_ref, part_theirs_ref,
):
    width = d_ref.shape[-1] // 3
    d_heads = dot(two_sides(mine_ref, theirs_ref), w_ref[:, 3 * width :], ROW).astype(BF16)
    qkv = qkv_ref[0]
    query, key, value = (qkv[:, i * width : (i + 1) * width] for i in range(3))
    same_doc = id_col[0] == id_row[0]
    d_query = d_key = d_value = jnp.zeros((qkv.shape[0], width), F32)
    for h, lanes in enumerate(head_lanes(width)):
        scores = head_scores(query, key, lanes, same_doc)
        probs = jnp.exp(scores - log_ref[0, :, h : h + 1])
        d_prob = dot(jnp.where(lanes, d_heads, jnp.zeros_like(d_heads)), value, COL)
        row_dot = jnp.sum(probs * d_prob, axis=1, keepdims=True)
        d_score = (probs * (d_prob - row_dot)).astype(BF16)
        d_query = jnp.where(lanes, dot(d_score, key, ROW), d_query)
        d_key = jnp.where(lanes, dot(d_score, query, DOWN), d_key)
        d_value = jnp.where(lanes, dot(probs.astype(BF16), d_heads, DOWN), d_value)
    d_query, d_key = d_query * SCALE, d_key * SCALE
    d_all = jnp.concatenate([d_query, d_key, d_value], 1).astype(BF16)
    d_ref[...] = d_all.reshape(d_ref.shape)
    part = dot(d_all, w_ref[:, : 3 * width], COL).astype(BF16)
    half = part.shape[0] // 2
    part_mine_ref[...] = part[:half].reshape(part_mine_ref.shape)
    part_theirs_ref[...] = part[half:].reshape(part_theirs_ref.shape)
    bias_ref[0, 0:1] = jnp.sum(d_query, axis=0, keepdims=True)
    bias_ref[0, 1:2] = jnp.sum(d_value, axis=0, keepdims=True)


def of_side(mine_ref, theirs_ref):
    return jnp.where(pl.program_id(0) < pl.num_programs(0) // 2, mine_ref[...], theirs_ref[...])


def to_side(values, mine_ref, theirs_ref):
    first = pl.program_id(0) < pl.num_programs(0) // 2

    @pl.when(first)
    def _():
        mine_ref[...] = values

    @pl.when(jnp.logical_not(first))
    def _():
        theirs_ref[...] = values


def ffn_kernel(
    hm_ref, ht_ref, wm_ref, wt_ref, xm_ref, xt_ref, gain_ref, shift_ref, up_ref, down_ref, bias_ref,
    hidden_ref, act_ref, slope_ref, part_mine_ref, part_theirs_ref, resid_ref,
):
    own = resid_ref.shape[0]
    x, parts = of_side(xm_ref, xt_ref), []
    for at in range(0, x.shape[0], CHUNK):
        rows = slice(at, at + CHUNK)
        attended = dot(hm_ref[rows], wm_ref[...], COL) + dot(ht_ref[rows], wt_ref[...], COL)
        resid = x[rows].astype(F32) + attended + shift_ref[0:1]
        if at == 0:

            @pl.when(pl.program_id(0) == 0)
            def _(resid=resid):
                resid_ref[...] = resid[:own]

        hidden = (normalise(resid)[0] * gain_ref[0:1] + shift_ref[1:2]).astype(BF16)
        hidden_ref[rows] = hidden
        pre_up = dot(hidden, up_ref[...], ROW) + bias_ref[...]
        cdf = 0.5 * (1.0 + lax.erf(pre_up * 0.5**0.5))
        activated = (pre_up * cdf).astype(BF16)
        act_ref[rows] = activated
        slope_ref[rows] = cdf + pre_up * jnp.exp(-0.5 * pre_up * pre_up) * 0.3989422804014327
        parts.append(dot(activated, down_ref[...], COL).astype(BF16))
    to_side(jnp.concatenate(parts, 0), part_mine_ref, part_theirs_ref)


def ffn_back_kernel(
    mine_ref, theirs_ref, slope_ref, up_ref, down_ref, d_ref, part_mine_ref, part_theirs_ref, sum_ref
):
    d_ffn, parts, sums = of_side(mine_ref, theirs_ref), [], []
    for at in range(0, d_ffn.shape[0], CHUNK):
        rows = slice(at, at + CHUNK)
        d_pre = dot(d_ffn[rows], down_ref[...], ROW) * slope_ref[rows]
        low = d_pre.astype(BF16)
        d_ref[rows] = low
        parts.append(dot(low, up_ref[...], COL).astype(BF16))
        sums.append(jnp.sum(d_pre, axis=0, keepdims=True))
    to_side(jnp.concatenate(parts, 0), part_mine_ref, part_theirs_ref)

    @pl.when(pl.program_id(0) == 0)
    def _():
        sum_ref[...] = jnp.zeros_like(sum_ref)

    sum_ref[...] += sum(sums)


def over_tokens(left_refs, right_ref):
    total, at = None, 0
    for ref in left_refs:
        rows = ref.shape[0]
        term = dot(ref[...], right_ref[at : at + rows], DOWN)
        total, at = term if total is None else total + term, at + rows
    return total


def weight_grads_kernel(count, n_in, here_ref, *refs):
    ins, outs = refs[:n_in], refs[n_in:]
    left = ins[: count + 2]
    first, second, right1, right2 = left[:count], left[count:], ins[count + 2], ins[count + 3]
    rows = left[0].shape[1]
    low1 = over_tokens(first, right1).astype(BF16)
    low2 = over_tokens(second, right2).astype(BF16)
    values = jnp.concatenate([low1, low2], 1)
    if n_in > count + 4:
        small = ins[-1][...]
        high = small.astype(BF16).astype(F32)
        packed = jnp.concatenate([high, small - high], 0).astype(BF16)
        values = jnp.concatenate([values, packed], 0)
    step = pl.program_id(0)
    if len(outs) == RING:
        places = [[(outs[i], 0, values.shape[0])] for i in range(RING)]
    else:
        half = rows // 2
        places = [[(outs[0], 0, rows)], [(outs[1], 0, rows)], [(outs[2], 0, half), (outs[3], half, rows)]]
        places.append([(outs[4], 0, rows)])
    for i in range(RING):

        @pl.when(step == i)
        def _(i=i):
            for out_ref, start, stop in places[i]:
                out_ref[...] = values[start:stop]


def weight_grads(first, second, right1, right2, small=None):
    width = second[0].shape[1]
    rows = width // RING
    cols = right1.shape[1] + right2.shape[1]
    lefts = list(first) + list(second)
    extra = 0 if small is None else 2 * small.shape[0]
    tail = [right1, right2] + ([] if small is None else [small])
    heights = [rows, rows, rows // 2, rows // 2, rows] if small is None else [rows + extra] * RING
    return pl.pallas_call(
        functools.partial(weight_grads_kernel, len(first), len(lefts) + len(tail)),
        out_shape=[jax.ShapeDtypeStruct((n, cols), BF16) for n in heights],
        grid_spec=pltpu.PrefetchScalarGridSpec(
            num_scalar_prefetch=1,
            grid=(RING,),
            in_specs=[
                pl.BlockSpec((v.shape[0], rows), lambda i, here: (0, (here[0] + i) % RING))
                for v in lefts
            ]
            + [pl.BlockSpec(v.shape, lambda i, here: (0, 0)) for v in tail],
            out_specs=[pl.BlockSpec((n, cols), lambda i, here: (0, 0)) for n in heights],
        ),
        cost_estimate=cost(5),
        compiler_params=pltpu.CompilerParams(vmem_limit_bytes=16 * MIB),
    )(lax.axis_index("z").astype(jnp.int32).reshape(1), *lefts, *tail)


def sum_refs(refs, rows):
    return same_sum([ref[rows].astype(F32) for ref in refs])


def packed_sum(refs, first):
    values = sum_refs(refs, slice(first, None))
    count = values.shape[0] // 2
    return values[:count] + values[count:]


def relay_kernel(here_ref, *refs):
    attn, small, ffn, outs = refs[:4], refs[4:8], refs[8:11], refs[11:]
    low = sum_refs(attn, slice(None)).astype(BF16)
    values = packed_sum(small, 0)
    high = values.astype(BF16).astype(F32)
    packed = jnp.concatenate([high, values - high], 0).astype(BF16)
    own, right, left = (ref[...].astype(F32) for ref in ffn)
    grad = (own + (right + left)).astype(BF16)
    cols = low.shape[1]
    cuts = [grad[:, i : i + cols] for i in range(0, grad.shape[1], cols)]
    message = jnp.concatenate([low, *cuts, packed], 0)
    for i, out_ref in enumerate(outs):

        @pl.when(pl.program_id(0) == i)
        def _(out_ref=out_ref):
            out_ref[...] = message


def relay(attn, ffn, rows):
    cols, extra = attn[0].shape[1], attn[0].shape[0] - RING * rows
    wide = ffn[0].shape[1]
    height = rows * (1 + wide // cols) + extra

    def turned(n):
        return pl.BlockSpec((rows, n), lambda i, here: ((here[0] + i) % RING, 0))

    below = pl.BlockSpec((extra, cols), lambda i, here: (RING * rows // extra, 0))
    return pl.pallas_call(
        relay_kernel,
        out_shape=[jax.ShapeDtypeStruct((height, cols), BF16)] * RING,
        grid_spec=pltpu.PrefetchScalarGridSpec(
            num_scalar_prefetch=1,
            grid=(RING,),
            in_specs=[turned(cols)] * RING + [below] * RING + [turned(wide)] * 3,
            out_specs=[pl.BlockSpec((height, cols), lambda i, here: (0, 0))] * RING,
        ),
        cost_estimate=cost(2),
        compiler_params=pltpu.CompilerParams(vmem_limit_bytes=16 * MIB),
    )(lax.axis_index("x").astype(jnp.int32).reshape(1), *attn, *attn, *ffn)


def outputs_kernel(a_ref, b_ref, c_ref, d_ref, qkv, out, up, down, heads, units, gain, move):
    refs = (a_ref, b_ref, c_ref, d_ref)
    rows, width = qkv.shape[1:]
    values = sum_refs(refs, slice(0, rows))
    for i in range(3):
        qkv[i] = values[:, i * width : (i + 1) * width]
    out[...] = values[:, 3 * width :].T
    up[...] = sum_refs(refs, slice(rows, 2 * rows))
    down[...] = sum_refs(refs, slice(2 * rows, 3 * rows)).T
    small = packed_sum(refs, 3 * rows)
    cols, count = small.shape[1], gain.shape[0] + move.shape[0]
    pieces = gain.shape[1] // cols
    for i in range(pieces):
        span = slice(i * cols, (i + 1) * cols)
        gain[:, span] = small[i * count : i * count + gain.shape[0]]
        move[:, span] = small[i * count + gain.shape[0] : (i + 1) * count]
    units[...] = small[pieces * count : pieces * count + 1]
    last = small[pieces * count + 1 : pieces * count + 2]
    heads[0:1] = last[:, :width]
    heads[1:2] = last[:, width : 2 * width]


def total_of(refs):
    own, other, first, second, third = (ref[...].astype(F32) for ref in refs)
    return (own + other) + first + second + third


def rows_of(values):
    return jnp.concatenate([jnp.sum(v, axis=0, keepdims=True) for v in values], 0)


def second_norm_kernel(
    own_ref, other_ref, a_ref, b_ref, c_ref, resid1_ref, cot_ref, gain_ref, shift_ref,
    result_ref, d_ref, low_ref, sum_ref,
):
    normed = normalise(resid1_ref[...])[0] * gain_ref[0:1] + shift_ref[1:2]
    resid2 = normed + total_of((own_ref, other_ref, a_ref, b_ref, c_ref)) + shift_ref[2:3]
    unit, inverse = normalise(resid2)
    result_ref[...] = (unit * gain_ref[1:2] + shift_ref[3:4]).astype(BF16)
    cot = cot_ref[...].astype(F32)
    d_resid2 = normalise_back(cot * gain_ref[1:2], unit, inverse)
    d_ref[...] = d_resid2
    low_ref[...] = d_resid2.astype(BF16)
    sum_ref[...] = rows_of([cot * unit, d_resid2, cot])


def first_norm_kernel(
    own_ref, other_ref, a_ref, b_ref, c_ref, resid1_ref, d_resid2_ref, gain_ref, sum_ref, d_ref, sent_ref
):
    rows = d_ref.shape[0]
    d_normed = d_resid2_ref[...] + total_of((own_ref, other_ref, a_ref, b_ref, c_ref))
    unit, inverse = normalise(resid1_ref[...])
    d_resid1 = normalise_back(d_normed * gain_ref[0:1], unit, inverse)
    d_ref[...] = d_resid1
    sent_ref[0:rows] = d_resid1.astype(BF16)
    one = rows_of([d_normed * unit, d_resid1, d_normed])
    two = sum_ref[...]
    sums = jnp.concatenate([one[0:1], two[0:1], one[1:3], two[1:3]], 0)
    high = sums.astype(BF16)
    low = (sums - high.astype(F32)).astype(BF16)
    room = jnp.zeros((4, sums.shape[1]), F32)
    packed = jnp.concatenate([high.astype(F32), low.astype(F32), room], 0)
    sent_ref[rows : rows + 16] = packed.astype(BF16)


def on_device(
    tokens,
    segment_ids,
    qkv_weight,
    out_weight,
    up_weight,
    down_weight,
    head_bias,
    up_bias,
    gains,
    shifts,
    cotangent,
):
    seqs, rows, width = tokens.shape
    length = segment_ids.shape[1]
    count = seqs * length
    own = seqs * rows
    head_width = qkv_weight.shape[2]
    units = up_weight.shape[1]
    heads = head_width // HEAD_DIM
    y = lax.axis_index("y")
    core = lax.axis_index("core")

    vmem = pl.BlockSpec(memory_space=pltpu.VMEM)
    packed_width = 4 * head_width + 2 * units
    weights = call(
        1,
        weights_kernel,
        [((qkv_weight.shape[1], packed_width), BF16)],
        in_specs=[vmem] * 4,
    )(qkv_weight, out_weight, up_weight, down_weight)[0]
    w_blocks = gather_direct(weights, "x")
    mine = tokens.reshape(own, width)
    one, three, *w_blocks = lax.optimization_barrier((shift(mine, "y", -1), shift(mine, "y", 1), *w_blocks))
    w_attn, w_ffn = by_index(w_blocks, "x", [4 * head_width, 2 * units])
    w_blocks = gather_direct(w_attn, "z")
    two = [shift(one[: own // 2], "y", -1), shift(three[own // 2 :], "y", 1)]
    *two, w_blocks[1], w_blocks[2], w_blocks[3] = lax.optimization_barrier((*two, *w_blocks[1:]))
    x_blocks = [mine, one, *two, three]
    w_attn = by_index(w_blocks, "z")

    ids = segment_ids.reshape(seqs, RING, 2, rows)
    ids = jnp.concatenate([ids, ids], 1)
    ids = lax.dynamic_slice_in_dim(ids, y, RING, 1)
    ids = jnp.where(core == 0, ids, ids[:, :, ::-1])
    ids = jnp.swapaxes(ids, 1, 2).reshape(seqs, length)
    ids = [ids[:, :, None], ids[:, None, :]]

    def by_seq(*block):
        return pl.BlockSpec(block, lambda s: tuple(s if n == 1 else 0 for n in block[:-2]) + (0, 0))

    def whole(*block):
        return pl.BlockSpec(block, lambda s: (0,) * len(block))

    side = by_seq(RING, 1, rows, width)
    id_specs = [
        pl.BlockSpec((1, length, 1), lambda s: (s, 0, 0)),
        pl.BlockSpec((1, 1, length), lambda s: (s, 0, 0)),
    ]

    def by_chip(sides):
        return [v.reshape(RING, seqs, rows, width) for v in sides]

    x_mine = assemble(x_blocks)
    x_sides = [x_mine, sibling(x_mine)]
    bias = jnp.concatenate([head_bias[0], jnp.zeros((head_width,), F32), head_bias[1]])
    qkv, head_out, log_total = call(
        4,
        attend_kernel,
        [
            ((seqs, length, 3 * head_width), BF16),
            ((2, RING, seqs, rows, head_width), BF16),
            ((seqs, length, heads), F32),
        ],
        (seqs,),
        [side, side, whole(width, 4 * head_width), whole(1, 3 * head_width)] + id_specs,
        [
            by_seq(1, length, 3 * head_width),
            by_seq(2, RING, 1, rows, head_width),
            by_seq(1, length, heads),
        ],
        mib=24,
    )(*by_chip(x_sides), w_attn, bias[None], *ids)
    head_out = head_out.reshape(count, head_width)
    w_blocks = gather_ring(after(w_ffn, head_out), "z")
    w_ffn = by_index(w_blocks, "z")
    heads_blocks = from_chips(jnp.concatenate([head_out, w_attn[:, 3 * head_width :]], 0))
    heads_blocks[3] = after(heads_blocks[3], w_blocks[2], w_blocks[3])
    heads_mine = call(
        1.5,
        heads_kernel,
        [((count + width, 4 * head_width), BF16)],
        in_specs=[vmem] * RING,
    )(*heads_blocks)[0]
    heads_theirs = sibling(heads_mine)
    token_blocks = 2
    half = count // 2

    def by_block(cols, turn=0, blocks=token_blocks):
        return pl.BlockSpec((count // token_blocks, cols), lambda i: ((i + turn) % blocks, 0))

    side_block = by_block(width, blocks=token_blocks // 2)
    side_parts = [
        pl.BlockSpec((count // token_blocks, width), lambda i: (jnp.minimum(i, token_blocks // 2 - 1), 0)),
        pl.BlockSpec((count // token_blocks, width), lambda i: (jnp.maximum(i - token_blocks // 2, 0), 0)),
    ]
    w_specs = [
        pl.BlockSpec((width, units), lambda i: (0, 0)),
        pl.BlockSpec((width, units), lambda i: (0, 1)),
    ]
    hidden, activated, slope, *part, resid1 = call(
        11,
        ffn_kernel,
        [
            ((count, width), BF16),
            ((count, units), BF16),
            ((count, units), F32),
            ((half, width), BF16),
            ((half, width), BF16),
            ((own, width), F32),
        ],
        (token_blocks,),
        [
            by_block(4 * head_width),
            by_block(4 * head_width, token_blocks // 2),
            pl.BlockSpec((width, 4 * head_width), lambda i: (1, 0)),
            pl.BlockSpec((width, 4 * head_width), lambda i: (1, 0)),
            side_block,
            side_block,
            whole(2, width),
            whole(4, width),
            *w_specs,
            whole(1, units),
        ],
        [by_block(width), by_block(units), by_block(units), *side_parts, whole(own, width)],
        mib=32,
    )(
        heads_mine, heads_theirs, heads_mine, heads_theirs, *x_sides, gains, shifts, w_ffn, w_ffn,
        up_bias[None],
    )
    total, low = scatter_sides(*part)
    part_specs = [pl.BlockSpec((own, width), lambda i: (0, 0))] * 2
    result, d_resid2, d_resid2_low, second_sums = call(
        1.4,
        second_norm_kernel,
        [((own, width), BF16), ((own, width), F32), ((own, width), BF16), ((3, width), F32)],
        grid=(1,),
        in_specs=part_specs + [vmem] * 7,
    )(*total, *scatter_chips(low), resid1, cotangent.reshape(own, width), gains, shifts)

    d_ffn = gather_tokens(d_resid2_low)
    d_pre, *part, unit_terms = call(
        5.5,
        ffn_back_kernel,
        [((count, units), BF16), ((half, width), BF16), ((half, width), BF16), ((1, units), F32)],
        (token_blocks,),
        [side_block, side_block, by_block(units), *w_specs],
        [by_block(units), *side_parts, whole(1, units)],
        mib=24,
    )(*d_ffn, slope, w_ffn, w_ffn)
    total, low = scatter_sides(*part)
    got = scatter_chips(low)
    grads = list(weight_grads([after(hidden, *low)], d_ffn, d_pre, activated))
    d_resid1, sent = call(
        0.7,
        first_norm_kernel,
        [((own, width), F32), ((own + 16, width), BF16)],
        grid=(1,),
        in_specs=part_specs + [vmem] * 7,
    )(*total, *got, resid1, d_resid2, gains, second_sums)

    blocks = from_chips(sent)
    ring = ring_first(grads, "z")
    packed = pack(same_sum([unpack(b[own:], 6) for b in blocks]), 16)
    mine = assemble([b[:own] for b in blocks])
    d_attn = [mine, sibling(mine)]
    norm_terms = unpack(packed, 6) + unpack(sibling(packed), 6)
    d_proj, bias_terms, *part = call(
        8,
        attend_back_kernel,
        [
            ((2, RING, seqs, rows, 3 * head_width), BF16),
            ((seqs, 2, head_width), F32),
            ((RING, seqs, rows, width), BF16),
            ((RING, seqs, rows, width), BF16),
        ],
        (seqs,),
        [side, side, whole(width, 4 * head_width)]
        + [by_seq(1, length, 3 * head_width), by_seq(1, length, heads)]
        + id_specs,
        [by_seq(2, RING, 1, rows, 3 * head_width), by_seq(1, 2, head_width), side, side],
        mib=32,
    )(*by_chip(d_attn), w_attn, qkv, log_total, *ids)
    grads = ring_second(grads, ring, "z")
    d_proj = d_proj.reshape(count, 3 * head_width)
    bias_terms = jnp.sum(bias_terms, 0)
    cols = 4 * head_width
    pieces = [norm_terms[:, i : i + cols] for i in range(0, width, cols)]
    pieces += [unit_terms.reshape(-1, cols), bias_terms.reshape(1, 2 * head_width)]
    pieces[-1] = jnp.pad(pieces[-1], ((0, 0), (0, cols - 2 * head_width)))
    small = jnp.concatenate(pieces, 0)
    small = jnp.pad(small, ((0, -small.shape[0] % 8), (0, 0)))
    messages = weight_grads(x_sides, d_attn, d_proj, head_out, small)
    messages = exchange(messages, "z")
    total, low = scatter_sides(*(p.reshape(half, width) for p in part))
    got = scatter_chips(low)
    grad_tokens = d_resid1 + total[0][:own].astype(F32) + total[1][:own].astype(F32)
    grad_tokens = grad_tokens + got[0].astype(F32) + got[1].astype(F32) + got[2].astype(F32)
    messages[3] = after(messages[3], got[0])
    messages = exchange(relay(messages, grads, rows), "x")
    weights_out = list(call(
        2,
        outputs_kernel,
        [
            ((3, rows, head_width), F32),
            ((head_width, rows), F32),
            ((rows, units), F32),
            ((units, rows), F32),
            ((2, head_width), F32),
            ((1, units), F32),
            ((2, width), F32),
            ((4, width), F32),
        ],
        in_specs=[vmem] * 4,
    )(*messages))
    weights_out[5] = weights_out[5].reshape(units)
    return (result.reshape(tokens.shape), grad_tokens.reshape(tokens.shape), *weights_out)


def solution(mesh):
    mesh = Mesh(mesh.devices.reshape(RING, RING, RING, 2), ("z", "x", "y", "core"))
    dp, mp = ("z", "x"), ("y", "core")
    in_specs = (
        P(dp, mp, None),
        P(dp, None),
        P(None, dp, mp),
        P(mp, dp),
        P(dp, mp),
        P(mp, dp),
        P(None, mp),
        P(mp),
        P(),
        P(),
        P(dp, mp, None),
    )
    out_specs = (
        P(dp, mp, None),
        P(dp, mp, None),
        P(None, dp, mp),
        P(mp, dp),
        P(dp, mp),
        P(mp, dp),
        P(None, mp),
        P(mp),
        P(),
        P(),
    )
    return jax.shard_map(
        on_device, mesh=mesh, in_specs=in_specs, out_specs=out_specs, check_vma=False
    )
```

```python
import functools

import jax
import jax.numpy as jnp
from jax import lax
from jax.experimental import pallas as pl
from jax.experimental.pallas import tpu as pltpu
from jax.sharding import Mesh
from jax.sharding import PartitionSpec as P

HEAD_DIM = 64
EPSILON = 1e-12
SCALE = HEAD_DIM ** (-0.5)
F32 = jnp.float32
BF16 = jnp.bfloat16
RING = 4
CHUNK = 256
MIB = 2**20


def shift(value, axis, step):
    return lax.ppermute(value, axis, [(i, (i + step) % RING) for i in range(RING)])


def sibling(value):
    return lax.ppermute(value, "core", [(0, 1), (1, 0)])


def assemble(blocks):
    return jnp.concatenate(blocks, 0)


def from_chips(rows):
    return [rows, shift(rows, "y", -1), shift(rows, "y", 2), shift(rows, "y", 1)]


def gather_tokens(rows):
    mine = assemble(from_chips(rows))
    return mine, sibling(mine)


def scatter_sides(mine, theirs):
    other = sibling(theirs)
    rows = mine.shape[0] // RING
    cuts = [slice(i * rows, (i + 1) * rows) for i in (1, 2, 3)]
    return [mine, other], [(mine[c].astype(F32) + other[c].astype(F32)).astype(BF16) for c in cuts]


def scatter_chips(low):
    return [shift(low[0], "y", 1), shift(low[1], "y", 2), shift(low[2], "y", -1)]


def after(value, *others):
    return lax.optimization_barrier((value, *others))[0]


def after_all(values, *others):
    return lax.optimization_barrier((*values, *others))[: len(values)]


def gather_direct(rows, axis):
    return [rows, shift(rows, axis, -1), shift(rows, axis, 2), shift(rows, axis, 1)]


def gather_ring(rows, axis):
    half = rows.shape[0] // 2
    one, three = shift(rows, axis, -1), shift(rows, axis, 1)
    low, high = shift(one[:half], axis, -1), shift(three[half:], axis, 1)
    return [rows, one, low, high, three]


def pack(values, rows):
    high = lax.reduce_precision(values, 8, 7)
    room = jnp.zeros((rows - 2 * values.shape[0], values.shape[1]), BF16)
    return jnp.concatenate([high.astype(BF16), (values - high).astype(BF16), room], 0)


def unpack(packed, count):
    return packed[:count].astype(F32) + packed[count : 2 * count].astype(F32)


def same_sum(terms):
    return (terms[0] + terms[2]) + (terms[1] + terms[3])


def exchange(messages, axis):
    return [
        messages[0],
        shift(messages[1], axis, 1),
        shift(messages[2], axis, 2),
        shift(messages[3], axis, -1),
    ]


def ring_first(blocks, axis):
    return shift(blocks[2], axis, 1), shift(blocks[3], axis, -1)


def ring_second(blocks, got, axis):
    low, high = got
    half = low.shape[0]
    right = (blocks[1][:half].astype(F32) + low.astype(F32)).astype(BF16)
    left = (blocks[4][half:].astype(F32) + high.astype(F32)).astype(BF16)
    right = shift(jnp.concatenate([right, blocks[1][half:]], 0), axis, 1)
    left = shift(jnp.concatenate([blocks[4][:half], left], 0), axis, -1)
    return blocks[0], right, left


def normalise(resid):
    centered = resid - jnp.mean(resid, axis=-1, keepdims=True)
    variance = jnp.mean(centered * centered, axis=-1, keepdims=True)
    inverse = lax.rsqrt(variance + EPSILON)
    return centered * inverse, inverse


def normalise_back(cot, unit, inverse):
    return (
        cot
        - jnp.mean(cot, axis=-1, keepdims=True)
        - unit * jnp.mean(cot * unit, axis=-1, keepdims=True)
    ) * inverse


def dot(left, right, dims):
    return lax.dot_general(left, right, ((dims[0], dims[1]), ((), ())), preferred_element_type=F32)


ROW, COL = ((1,), (0,)), ((1,), (1,))
DOWN = ((0,), (0,))


def cost(micros):
    return pl.CostEstimate(flops=int(micros * 1.15e9), bytes_accessed=2**20, transcendentals=0)


def call(micros, kernel, outs, grid=(), in_specs=None, out_specs=None, mib=16):
    whole = pl.BlockSpec(memory_space=pltpu.VMEM)
    return pl.pallas_call(
        kernel,
        out_shape=[jax.ShapeDtypeStruct(shape, dtype) for shape, dtype in outs],
        grid=grid,
        in_specs=in_specs,
        out_specs=out_specs or [whole] * len(outs),
        cost_estimate=cost(micros),
        compiler_params=pltpu.CompilerParams(vmem_limit_bytes=mib * MIB),
    )


def weights_kernel(qkv_ref, out_ref, up_ref, down_ref, packed_ref):
    rest = [out_ref[...], up_ref[...], down_ref[...]]
    packed_ref[...] = jnp.concatenate([qkv_ref[0], qkv_ref[1], qkv_ref[2], *rest], 1)


def by_index_kernel(count, here_ref, *refs):
    blocks, outs = refs[:count], refs[count:]
    rows = blocks[0].shape[0]
    at = 0
    for ref in blocks:
        index = (here_ref[0] + at // rows) % RING
        start = pl.multiple_of(index * rows + at % rows, 16)
        at += ref.shape[0]
        left = 0
        for out_ref in outs:
            cols = out_ref.shape[1]
            out_ref[pl.ds(start, ref.shape[0]), :] = ref[:, left : left + cols]
            left += cols


def by_index(blocks, axis, cuts=None):
    rows, cols = blocks[0].shape
    vmem = pl.BlockSpec(memory_space=pltpu.VMEM)
    outs = [(RING * rows, n) for n in cuts or [cols]]
    found = pl.pallas_call(
        functools.partial(by_index_kernel, len(blocks)),
        out_shape=[jax.ShapeDtypeStruct(shape, BF16) for shape in outs],
        grid_spec=pltpu.PrefetchScalarGridSpec(
            num_scalar_prefetch=1,
            grid=(1,),
            in_specs=[vmem] * len(blocks),
            out_specs=[vmem] * len(outs),
        ),
        cost_estimate=cost(1),
        compiler_params=pltpu.CompilerParams(vmem_limit_bytes=16 * MIB),
    )(lax.axis_index(axis).astype(jnp.int32).reshape(1), *blocks)
    return found if cuts else found[0]


def head_lanes(width):
    lane = lax.broadcasted_iota(jnp.int32, (1, width), 1)
    return [(lane // HEAD_DIM) == h for h in range(width // HEAD_DIM)]


def heads_kernel(*refs):
    *blocks, out_ref = refs
    width = blocks[0].shape[1]
    count = out_ref.shape[0] // 2
    rows = count // 2 // RING
    for j, ref in enumerate([blocks[0], blocks[1], None, blocks[4]]):
        cols = slice(j * width, (j + 1) * width)
        if ref is None:
            ref = blocks[2]
            out_ref[count:, cols] = blocks[3][...]
        else:
            out_ref[count:, cols] = ref[count:]
        for at in range(0, count, count // 2):
            cut = (RING - j) * rows
            if j:
                out_ref[at : at + j * rows, cols] = ref[at + cut : at + count // 2]
            out_ref[at + j * rows : at + count // 2, cols] = ref[at : at + cut]


def two_sides(mine_ref, theirs_ref):
    width = mine_ref.shape[-1]
    return jnp.concatenate(
        [mine_ref[...].reshape(-1, width), theirs_ref[...].reshape(-1, width)], 0
    )


def head_scores(query, key, lanes, same_doc):
    query = jnp.where(lanes, query, jnp.zeros_like(query))
    return jnp.where(same_doc, dot(query, key, COL) * SCALE, -1e30)


def attend_kernel(mine_ref, theirs_ref, w_ref, bias_ref, id_col, id_row, qkv_ref, out_ref, log_ref):
    width = out_ref.shape[-1]
    projected = dot(two_sides(mine_ref, theirs_ref), w_ref[:, : 3 * width], ROW)
    qkv = (projected + bias_ref[...]).astype(BF16)
    qkv_ref[0] = qkv
    query, key, value = (qkv[:, i * width : (i + 1) * width] for i in range(3))
    same_doc = id_col[0] == id_row[0]
    out = jnp.zeros((qkv.shape[0], width), F32)
    for h, lanes in enumerate(head_lanes(width)):
        scores = head_scores(query, key, lanes, same_doc)
        top = jnp.max(scores, axis=1, keepdims=True)
        weight = jnp.exp(scores - top)
        total = jnp.sum(weight, axis=1, keepdims=True)
        log_ref[0, :, h : h + 1] = top + jnp.log(total)
        low = (weight * (1.0 / total)).astype(BF16)
        out = jnp.where(lanes, dot(low, value, ROW), out)
    out_ref[...] = out.astype(BF16).reshape(out_ref.shape)


def attend_back_kernel(
    mine_ref, theirs_ref, w_ref, qkv_ref, log_ref, id_col, id_row,
    d_ref, bias_ref, part_mine_ref, part_theirs_ref,
):
    width = d_ref.shape[-1] // 3
    d_heads = dot(two_sides(mine_ref, theirs_ref), w_ref[:, 3 * width :], ROW).astype(BF16)
    qkv = qkv_ref[0]
    query, key, value = (qkv[:, i * width : (i + 1) * width] for i in range(3))
    same_doc = id_col[0] == id_row[0]
    d_query = d_key = d_value = jnp.zeros((qkv.shape[0], width), F32)
    for h, lanes in enumerate(head_lanes(width)):
        scores = head_scores(query, key, lanes, same_doc)
        probs = jnp.exp(scores - log_ref[0, :, h : h + 1])
        d_prob = dot(jnp.where(lanes, d_heads, jnp.zeros_like(d_heads)), value, COL)
        row_dot = jnp.sum(probs * d_prob, axis=1, keepdims=True)
        d_score = (probs * (d_prob - row_dot)).astype(BF16)
        d_query = jnp.where(lanes, dot(d_score, key, ROW), d_query)
        d_key = jnp.where(lanes, dot(d_score, query, DOWN), d_key)
        d_value = jnp.where(lanes, dot(probs.astype(BF16), d_heads, DOWN), d_value)
    d_query, d_key = d_query * SCALE, d_key * SCALE
    d_all = jnp.concatenate([d_query, d_key, d_value], 1).astype(BF16)
    d_ref[...] = d_all.reshape(d_ref.shape)
    part = dot(d_all, w_ref[:, : 3 * width], COL).astype(BF16)
    half = part.shape[0] // 2
    part_mine_ref[...] = part[:half].reshape(part_mine_ref.shape)
    part_theirs_ref[...] = part[half:].reshape(part_theirs_ref.shape)
    bias_ref[0, 0:1] = jnp.sum(d_query, axis=0, keepdims=True)
    bias_ref[0, 1:2] = jnp.sum(d_value, axis=0, keepdims=True)


def ffn_kernel(
    hm_ref, ht_ref, wm_ref, wt_ref, x_ref, gain_ref, shift_ref, up_ref, down_ref, bias_ref,
    hidden_ref, act_ref, slope_ref, part_ref, resid_ref,
):
    for at in range(0, x_ref.shape[0], CHUNK):
        rows = slice(at, at + CHUNK)
        attended = dot(hm_ref[rows], wm_ref[...], COL) + dot(ht_ref[rows], wt_ref[...], COL)
        resid = x_ref[rows].astype(F32) + attended + shift_ref[0:1]
        if at == 0:
            resid_ref[...] = resid[: resid_ref.shape[0]]
        hidden = (normalise(resid)[0] * gain_ref[0:1] + shift_ref[1:2]).astype(BF16)
        hidden_ref[rows] = hidden
        pre_up = dot(hidden, up_ref[...], ROW) + bias_ref[...]
        cdf = 0.5 * (1.0 + lax.erf(pre_up * 0.5**0.5))
        activated = (pre_up * cdf).astype(BF16)
        act_ref[rows] = activated
        slope_ref[rows] = cdf + pre_up * jnp.exp(-0.5 * pre_up * pre_up) * 0.3989422804014327
        part_ref[rows] = dot(activated, down_ref[...], COL).astype(BF16)


def ffn_back_kernel(d_ffn_ref, slope_ref, up_ref, down_ref, d_ref, part_ref, sum_ref):
    sums = []
    for at in range(0, d_ffn_ref.shape[0], CHUNK):
        rows = slice(at, at + CHUNK)
        d_pre = dot(d_ffn_ref[rows], down_ref[...], ROW) * slope_ref[rows]
        low = d_pre.astype(BF16)
        d_ref[rows] = low
        part_ref[rows] = dot(low, up_ref[...], COL).astype(BF16)
        sums.append(jnp.sum(d_pre, axis=0, keepdims=True))
    sum_ref[...] = sum(sums)


def over_tokens(left_refs, right_refs):
    total, at = None, 0
    for i, ref in enumerate(left_refs):
        rows = ref.shape[0]
        right = right_refs[0][at : at + rows] if len(right_refs) == 1 else right_refs[i][...]
        term = dot(ref[...], right, DOWN)
        total, at = term if total is None else total + term, at + rows
    return total


def weight_grads_kernel(counts, n_in, here_ref, *refs):
    ins, outs = list(refs[:n_in]), refs[n_in:]
    first, second, right1, right2 = ([ins.pop(0) for _ in range(n)] for n in counts)
    rows = first[0].shape[1]
    low1 = over_tokens(first, right1).astype(BF16)
    low2 = over_tokens(second, right2).astype(BF16)
    values = jnp.concatenate([low1, low2], 1)
    if ins:
        small = ins[0][...]
        high = small.astype(BF16).astype(F32)
        packed = jnp.concatenate([high, small - high], 0).astype(BF16)
        values = jnp.concatenate([values, packed], 0)
    step = pl.program_id(0)
    if len(outs) == RING:
        places = [[(outs[i], 0, values.shape[0])] for i in range(RING)]
    else:
        half = rows // 2
        places = [[(outs[0], 0, rows)], [(outs[1], 0, rows)], [(outs[2], 0, half), (outs[3], half, rows)]]
        places.append([(outs[4], 0, rows)])
    for i in range(RING):

        @pl.when(step == i)
        def _(i=i):
            for out_ref, start, stop in places[i]:
                out_ref[...] = values[start:stop]


def weight_grads(first, second, right1, right2, small=None, mib=16):
    width = second[0].shape[1]
    rows = width // RING
    cols = right1[0].shape[1] + right2[0].shape[1]
    lefts = [*first, *second]
    counts = [len(v) for v in (first, second, right1, right2)]
    extra = 0 if small is None else 2 * small.shape[0]
    tail = [*right1, *right2] + ([] if small is None else [small])
    heights = [rows, rows, rows // 2, rows // 2, rows] if small is None else [rows + extra] * RING
    return pl.pallas_call(
        functools.partial(weight_grads_kernel, counts, len(lefts) + len(tail)),
        out_shape=[jax.ShapeDtypeStruct((n, cols), BF16) for n in heights],
        grid_spec=pltpu.PrefetchScalarGridSpec(
            num_scalar_prefetch=1,
            grid=(RING,),
            in_specs=[
                pl.BlockSpec((v.shape[0], rows), lambda i, here: (0, (here[0] + i) % RING))
                for v in lefts
            ]
            + [pl.BlockSpec(v.shape, lambda i, here: (0, 0)) for v in tail],
            out_specs=[pl.BlockSpec((n, cols), lambda i, here: (0, 0)) for n in heights],
        ),
        cost_estimate=cost(5),
        compiler_params=pltpu.CompilerParams(vmem_limit_bytes=mib * MIB),
    )(lax.axis_index("z").astype(jnp.int32).reshape(1), *lefts, *tail)


def sum_refs(refs, rows):
    return same_sum([ref[rows].astype(F32) for ref in refs])


def packed_sum(refs, first):
    values = sum_refs(refs, slice(first, None))
    count = values.shape[0] // 2
    return values[:count] + values[count:]


def relay_kernel(here_ref, *refs):
    attn, small, ffn, outs = refs[:4], refs[4:8], refs[8:11], refs[11:]
    low = sum_refs(attn, slice(None)).astype(BF16)
    values = packed_sum(small, 0)
    high = values.astype(BF16).astype(F32)
    packed = jnp.concatenate([high, values - high], 0).astype(BF16)
    own, right, left = (ref[...].astype(F32) for ref in ffn)
    grad = (own + (right + left)).astype(BF16)
    cols = low.shape[1]
    cuts = [grad[:, i : i + cols] for i in range(0, grad.shape[1], cols)]
    message = jnp.concatenate([low, *cuts, packed], 0)
    for i, out_ref in enumerate(outs):

        @pl.when(pl.program_id(0) == i)
        def _(out_ref=out_ref):
            out_ref[...] = message


def relay(attn, ffn, rows):
    cols, extra = attn[0].shape[1], attn[0].shape[0] - RING * rows
    wide = ffn[0].shape[1]
    height = rows * (1 + wide // cols) + extra

    def turned(n):
        return pl.BlockSpec((rows, n), lambda i, here: ((here[0] + i) % RING, 0))

    below = pl.BlockSpec((extra, cols), lambda i, here: (RING * rows // extra, 0))
    return pl.pallas_call(
        relay_kernel,
        out_shape=[jax.ShapeDtypeStruct((height, cols), BF16)] * RING,
        grid_spec=pltpu.PrefetchScalarGridSpec(
            num_scalar_prefetch=1,
            grid=(RING,),
            in_specs=[turned(cols)] * RING + [below] * RING + [turned(wide)] * 3,
            out_specs=[pl.BlockSpec((height, cols), lambda i, here: (0, 0))] * RING,
        ),
        cost_estimate=cost(2),
        compiler_params=pltpu.CompilerParams(vmem_limit_bytes=16 * MIB),
    )(lax.axis_index("x").astype(jnp.int32).reshape(1), *attn, *attn, *ffn)


def outputs_kernel(a_ref, b_ref, c_ref, d_ref, qkv, out, up, down, heads, units, gain, move):
    refs = (a_ref, b_ref, c_ref, d_ref)
    rows, width = qkv.shape[1:]
    values = sum_refs(refs, slice(0, rows))
    for i in range(3):
        qkv[i] = values[:, i * width : (i + 1) * width]
    out[...] = values[:, 3 * width :]
    up[...] = sum_refs(refs, slice(rows, 2 * rows))
    down[...] = sum_refs(refs, slice(2 * rows, 3 * rows))
    small = packed_sum(refs, 3 * rows)
    cols, count = small.shape[1], gain.shape[0] + move.shape[0]
    pieces = gain.shape[1] // cols
    for i in range(pieces):
        span = slice(i * cols, (i + 1) * cols)
        gain[:, span] = small[i * count : i * count + gain.shape[0]]
        move[:, span] = small[i * count + gain.shape[0] : (i + 1) * count]
    units[...] = small[pieces * count : pieces * count + 1]
    last = small[pieces * count + 1 : pieces * count + 2]
    heads[0:1] = last[:, :width]
    heads[1:2] = last[:, width : 2 * width]


def total_of(refs):
    own, other, first, second, third = (ref[...].astype(F32) for ref in refs)
    return (own + other) + first + second + third


def rows_of(values):
    return jnp.concatenate([jnp.sum(v, axis=0, keepdims=True) for v in values], 0)


def second_norm_kernel(
    own_ref, other_ref, a_ref, b_ref, c_ref, resid1_ref, cot_ref, gain_ref, shift_ref,
    result_ref, d_ref, low_ref, sum_ref,
):
    normed = normalise(resid1_ref[...])[0] * gain_ref[0:1] + shift_ref[1:2]
    resid2 = normed + total_of((own_ref, other_ref, a_ref, b_ref, c_ref)) + shift_ref[2:3]
    unit, inverse = normalise(resid2)
    result_ref[...] = (unit * gain_ref[1:2] + shift_ref[3:4]).astype(BF16)
    cot = cot_ref[...].astype(F32)
    d_resid2 = normalise_back(cot * gain_ref[1:2], unit, inverse)
    d_ref[...] = d_resid2
    low_ref[...] = d_resid2.astype(BF16)
    sum_ref[...] = rows_of([cot * unit, d_resid2, cot])


def first_norm_kernel(
    own_ref, other_ref, a_ref, b_ref, c_ref, resid1_ref, d_resid2_ref, gain_ref, sum_ref, d_ref, sent_ref
):
    rows = d_ref.shape[0]
    d_normed = d_resid2_ref[...] + total_of((own_ref, other_ref, a_ref, b_ref, c_ref))
    unit, inverse = normalise(resid1_ref[...])
    d_resid1 = normalise_back(d_normed * gain_ref[0:1], unit, inverse)
    d_ref[...] = d_resid1
    sent_ref[0:rows] = d_resid1.astype(BF16)
    one = rows_of([d_normed * unit, d_resid1, d_normed])
    two = sum_ref[...]
    sums = jnp.concatenate([one[0:1], two[0:1], one[1:3], two[1:3]], 0)
    high = sums.astype(BF16)
    low = (sums - high.astype(F32)).astype(BF16)
    room = jnp.zeros((4, sums.shape[1]), F32)
    packed = jnp.concatenate([high.astype(F32), low.astype(F32), room], 0)
    sent_ref[rows : rows + 16] = packed.astype(BF16)


def on_device(
    tokens,
    segment_ids,
    qkv_weight,
    out_weight,
    up_weight,
    down_weight,
    head_bias,
    up_bias,
    gains,
    shifts,
    cotangent,
):
    seqs, rows, width = tokens.shape
    length = segment_ids.shape[1]
    count = seqs * length
    own = seqs * rows
    head_width = qkv_weight.shape[2]
    units = up_weight.shape[1]
    heads = head_width // HEAD_DIM
    y = lax.axis_index("y")
    core = lax.axis_index("core")

    vmem = pl.BlockSpec(memory_space=pltpu.VMEM)
    packed_width = 4 * head_width + 2 * units
    weights = call(
        1,
        weights_kernel,
        [((qkv_weight.shape[1], packed_width), BF16)],
        in_specs=[vmem] * 4,
        mib=60,
    )(qkv_weight, out_weight.T, up_weight, down_weight.T)[0]
    w_blocks = gather_direct(weights, "x")
    mine = tokens.reshape(own, width)
    one, three, *w_blocks = lax.optimization_barrier((shift(mine, "y", -1), shift(mine, "y", 1), *w_blocks))
    w_attn, w_ffn = by_index(w_blocks, "x", [4 * head_width, 2 * units])
    w_blocks = gather_direct(w_attn, "z")
    two = [shift(one[: own // 2], "y", -1), shift(three[own // 2 :], "y", 1)]
    *two, w_blocks[1], w_blocks[2], w_blocks[3] = lax.optimization_barrier((*two, *w_blocks[1:]))
    x_blocks = [mine, one, *two, three]
    w_attn = by_index(w_blocks, "z")

    ids = segment_ids.reshape(seqs, RING, 2, rows)
    ids = jnp.concatenate([ids, ids], 1)
    ids = lax.dynamic_slice_in_dim(ids, y, RING, 1)
    ids = jnp.where(core == 0, ids, ids[:, :, ::-1])
    ids = jnp.swapaxes(ids, 1, 2).reshape(seqs, length)
    ids = [ids[:, :, None], ids[:, None, :]]

    def by_seq(*block):
        return pl.BlockSpec(block, lambda s: tuple(s if n == 1 else 0 for n in block[:-2]) + (0, 0))

    def whole(*block):
        return pl.BlockSpec(block, lambda s: (0,) * len(block))

    side = by_seq(RING, 1, rows, width)
    id_specs = [
        pl.BlockSpec((1, length, 1), lambda s: (s, 0, 0)),
        pl.BlockSpec((1, 1, length), lambda s: (s, 0, 0)),
    ]

    def by_chip(sides):
        return [v.reshape(RING, seqs, rows, width) for v in sides]

    x_mine = assemble(x_blocks)
    x_sides = [x_mine, sibling(x_mine)]
    bias = jnp.concatenate([head_bias[0], jnp.zeros((head_width,), F32), head_bias[1]])
    qkv, head_out, log_total = call(
        4,
        attend_kernel,
        [
            ((seqs, length, 3 * head_width), BF16),
            ((2, RING, seqs, rows, head_width), BF16),
            ((seqs, length, heads), F32),
        ],
        (seqs,),
        [side, side, whole(width, 4 * head_width), whole(1, 3 * head_width)] + id_specs,
        [
            by_seq(1, length, 3 * head_width),
            by_seq(2, RING, 1, rows, head_width),
            by_seq(1, length, heads),
        ],
        mib=24,
    )(*by_chip(x_sides), w_attn, bias[None], *ids)
    head_out = head_out.reshape(count, head_width)
    w_ffn = after(w_ffn, head_out)
    heads_own = jnp.concatenate([head_out, w_attn[:, 3 * head_width :]], 0)
    one, three, w_one, w_three = lax.optimization_barrier(
        (shift(heads_own, "y", -1), shift(heads_own, "y", 1), shift(w_ffn, "z", -1), shift(w_ffn, "z", 1))
    )
    two = lax.optimization_barrier(
        (
            shift(one[: heads_own.shape[0] // 2], "y", -1),
            shift(three[heads_own.shape[0] // 2 :], "y", 1),
            shift(w_one[: w_ffn.shape[0] // 2], "z", -1),
            shift(w_three[w_ffn.shape[0] // 2 :], "z", 1),
        )
    )
    heads_blocks = [heads_own, one, two[0], two[1], three]
    w_ffn = by_index([w_ffn, w_one, two[2], two[3], w_three], "z")
    heads_mine = call(
        1.5,
        heads_kernel,
        [((count + width, 4 * head_width), BF16)],
        in_specs=[vmem] * 5,
    )(*heads_blocks)[0]
    heads_theirs = sibling(heads_mine)
    half = count // 2

    def rows_at(place, height, cols, left=0):
        return pl.BlockSpec((height, cols), lambda i: (place, left))

    w_specs = [rows_at(0, width, units), rows_at(0, width, units, 1)]
    ffn = []
    for which in (1, 0):
        ffn.append(
            call(
                4,
                ffn_kernel,
                [
                    ((half, width), BF16),
                    ((half, units), BF16),
                    ((half, units), F32),
                    ((half, width), BF16),
                    ((own, width), F32),
                ],
                (1,),
                [
                    rows_at(which, half, 4 * head_width),
                    rows_at(1 - which, half, 4 * head_width),
                    rows_at(1, width, 4 * head_width),
                    rows_at(1, width, 4 * head_width),
                    vmem,
                    vmem,
                    vmem,
                    *w_specs,
                    vmem,
                ],
                mib=32,
            )(
                heads_mine, heads_theirs, heads_mine, heads_theirs, x_sides[which], gains, shifts,
                w_ffn, w_ffn, up_bias[None],
            )
        )
    hidden, activated, slope, part, resid1 = zip(*ffn[::-1])
    resid1 = resid1[0]
    total, low = scatter_sides(*part)
    part_specs = [pl.BlockSpec((own, width), lambda i: (0, 0))] * 2
    result, d_resid2, d_resid2_low, second_sums = call(
        1.4,
        second_norm_kernel,
        [((own, width), BF16), ((own, width), F32), ((own, width), BF16), ((3, width), F32)],
        grid=(1,),
        in_specs=part_specs + [vmem] * 7,
    )(*total, *scatter_chips(low), resid1, cotangent.reshape(own, width), gains, shifts)

    d_ffn = gather_tokens(d_resid2_low)
    ffn = [
        call(
            1.7,
            ffn_back_kernel,
            [((half, units), BF16), ((half, width), BF16), ((1, units), F32)],
            (1,),
            [vmem, vmem, *w_specs],
            mib=24,
        )(d, s, w_ffn, w_ffn)
        for d, s in zip(d_ffn, slope)
    ]
    d_pre, part, unit_terms = zip(*ffn)
    unit_terms = unit_terms[0] + unit_terms[1]
    total, low = scatter_sides(*part)
    got = scatter_chips(low)
    grads = list(weight_grads(after_all(hidden, *low), d_ffn, d_pre, activated))
    d_resid1, sent = call(
        0.7,
        first_norm_kernel,
        [((own, width), F32), ((own + 16, width), BF16)],
        grid=(1,),
        in_specs=part_specs + [vmem] * 7,
    )(*total, *got, resid1, d_resid2, gains, second_sums)

    ring = ring_first(grads, "z")
    blocks = from_chips(after(sent, *ring))
    packed = pack(same_sum([unpack(b[own:], 6) for b in blocks]), 16)
    mine = assemble([b[:own] for b in blocks])
    d_attn = [mine, sibling(mine)]
    norm_terms = unpack(packed, 6) + unpack(sibling(packed), 6)
    d_proj, bias_terms, *part = call(
        8,
        attend_back_kernel,
        [
            ((2, RING, seqs, rows, 3 * head_width), BF16),
            ((seqs, 2, head_width), F32),
            ((RING, seqs, rows, width), BF16),
            ((RING, seqs, rows, width), BF16),
        ],
        (seqs,),
        [side, side, whole(width, 4 * head_width)]
        + [by_seq(1, length, 3 * head_width), by_seq(1, length, heads)]
        + id_specs,
        [by_seq(2, RING, 1, rows, 3 * head_width), by_seq(1, 2, head_width), side, side],
        mib=32,
    )(*by_chip(d_attn), w_attn, qkv, log_total, *ids)
    grads = ring_second(grads, ring, "z")
    d_proj = d_proj.reshape(count, 3 * head_width)
    bias_terms = jnp.sum(bias_terms, 0)
    cols = 4 * head_width
    pieces = [norm_terms[:, i : i + cols] for i in range(0, width, cols)]
    pieces += [unit_terms.reshape(-1, cols), bias_terms.reshape(1, 2 * head_width)]
    pieces[-1] = jnp.pad(pieces[-1], ((0, 0), (0, cols - 2 * head_width)))
    small = jnp.concatenate(pieces, 0)
    small = jnp.pad(small, ((0, -small.shape[0] % 8), (0, 0)))
    messages = weight_grads(x_sides, d_attn, [d_proj], [head_out], small, 60)
    messages = exchange(messages, "z")
    total, low = scatter_sides(*(p.reshape(half, width) for p in part))
    got = scatter_chips(low)
    grad_tokens = d_resid1 + total[0][:own].astype(F32) + total[1][:own].astype(F32)
    grad_tokens = grad_tokens + got[0].astype(F32) + got[1].astype(F32) + got[2].astype(F32)
    messages[3] = after(messages[3], got[0])
    messages = exchange(relay(messages, grads, rows), "x")
    weights_out = list(call(
        2,
        outputs_kernel,
        [
            ((3, rows, head_width), F32),
            ((rows, head_width), F32),
            ((rows, units), F32),
            ((rows, units), F32),
            ((2, head_width), F32),
            ((1, units), F32),
            ((2, width), F32),
            ((4, width), F32),
        ],
        in_specs=[vmem] * 4,
    )(*messages))
    weights_out[1] = weights_out[1].T
    weights_out[3] = weights_out[3].T
    weights_out[5] = weights_out[5].reshape(units)
    return (result.reshape(tokens.shape), grad_tokens.reshape(tokens.shape), *weights_out)


def solution(mesh):
    mesh = Mesh(mesh.devices.reshape(RING, RING, RING, 2), ("z", "x", "y", "core"))
    dp, mp = ("z", "x"), ("y", "core")
    in_specs = (
        P(dp, mp, None),
        P(dp, None),
        P(None, dp, mp),
        P(mp, dp),
        P(dp, mp),
        P(mp, dp),
        P(None, mp),
        P(mp),
        P(),
        P(),
        P(dp, mp, None),
    )
    out_specs = (
        P(dp, mp, None),
        P(dp, mp, None),
        P(None, dp, mp),
        P(mp, dp),
        P(dp, mp),
        P(mp, dp),
        P(None, mp),
        P(mp),
        P(),
        P(),
    )
    return jax.shard_map(
        on_device, mesh=mesh, in_specs=in_specs, out_specs=out_specs, check_vma=False
    )
```

```python
import functools

import jax
import jax.numpy as jnp
from jax import lax
from jax.experimental import pallas as pl
from jax.experimental.pallas import tpu as pltpu
from jax.sharding import Mesh
from jax.sharding import PartitionSpec as P

HEAD_DIM = 64
EPSILON = 1e-12
SCALE = HEAD_DIM ** (-0.5)
F32 = jnp.float32
BF16 = jnp.bfloat16
RING = 4
CHUNK = 256
MIB = 2**20


def shift(value, axis, step):
    return lax.ppermute(value, axis, [(i, (i + step) % RING) for i in range(RING)])


def sibling(value):
    return lax.ppermute(value, "core", [(0, 1), (1, 0)])


def assemble(blocks):
    return jnp.concatenate(blocks, 0)


def from_chips(rows):
    return [rows, shift(rows, "y", -1), shift(rows, "y", 2), shift(rows, "y", 1)]


def gather_tokens(rows):
    mine = assemble(from_chips(rows))
    return mine, sibling(mine)


def scatter_sides(mine, theirs):
    other = sibling(theirs)
    rows = mine.shape[0] // RING
    cuts = [slice(i * rows, (i + 1) * rows) for i in (1, 2, 3)]
    return [mine, other], [(mine[c].astype(F32) + other[c].astype(F32)).astype(BF16) for c in cuts]


def scatter_chips(low):
    return [shift(low[0], "y", 1), shift(low[1], "y", 2), shift(low[2], "y", -1)]


def after(value, *others):
    return lax.optimization_barrier((value, *others))[0]


def after_all(values, *others):
    return lax.optimization_barrier((*values, *others))[: len(values)]


def gather_direct(rows, axis):
    return [rows, shift(rows, axis, -1), shift(rows, axis, 2), shift(rows, axis, 1)]


def gather_ring(rows, axis):
    half = rows.shape[0] // 2
    one, three = shift(rows, axis, -1), shift(rows, axis, 1)
    low, high = shift(one[:half], axis, -1), shift(three[half:], axis, 1)
    return [rows, one, low, high, three]


def pack(values, rows):
    high = lax.reduce_precision(values, 8, 7)
    room = jnp.zeros((rows - 2 * values.shape[0], values.shape[1]), BF16)
    return jnp.concatenate([high.astype(BF16), (values - high).astype(BF16), room], 0)


def unpack(packed, count):
    return packed[:count].astype(F32) + packed[count : 2 * count].astype(F32)


def same_sum(terms):
    return (terms[0] + terms[2]) + (terms[1] + terms[3])


def exchange(messages, axis):
    return [
        messages[0],
        shift(messages[1], axis, 1),
        shift(messages[2], axis, 2),
        shift(messages[3], axis, -1),
    ]


def ring_first(blocks, axis):
    return shift(blocks[2], axis, 1), shift(blocks[3], axis, -1)


def ring_second(blocks, got, axis):
    low, high = got
    half = low.shape[0]
    right = (blocks[1][:half].astype(F32) + low.astype(F32)).astype(BF16)
    left = (blocks[4][half:].astype(F32) + high.astype(F32)).astype(BF16)
    right = shift(jnp.concatenate([right, blocks[1][half:]], 0), axis, 1)
    left = shift(jnp.concatenate([blocks[4][:half], left], 0), axis, -1)
    return blocks[0], right, left


def normalise(resid):
    centered = resid - jnp.mean(resid, axis=-1, keepdims=True)
    variance = jnp.mean(centered * centered, axis=-1, keepdims=True)
    inverse = lax.rsqrt(variance + EPSILON)
    return centered * inverse, inverse


def normalise_back(cot, unit, inverse):
    return (
        cot
        - jnp.mean(cot, axis=-1, keepdims=True)
        - unit * jnp.mean(cot * unit, axis=-1, keepdims=True)
    ) * inverse


def dot(left, right, dims):
    return lax.dot_general(left, right, ((dims[0], dims[1]), ((), ())), preferred_element_type=F32)


ROW, COL = ((1,), (0,)), ((1,), (1,))
DOWN = ((0,), (0,))


def cost(micros):
    return pl.CostEstimate(flops=int(micros * 1.15e9), bytes_accessed=2**20, transcendentals=0)


def call(micros, kernel, outs, grid=(), in_specs=None, out_specs=None, mib=16):
    whole = pl.BlockSpec(memory_space=pltpu.VMEM)
    return pl.pallas_call(
        kernel,
        out_shape=[jax.ShapeDtypeStruct(shape, dtype) for shape, dtype in outs],
        grid=grid,
        in_specs=in_specs,
        out_specs=out_specs or [whole] * len(outs),
        cost_estimate=cost(micros),
        compiler_params=pltpu.CompilerParams(vmem_limit_bytes=mib * MIB),
    )


def weights_kernel(qkv_ref, out_ref, up_ref, down_ref, packed_ref):
    rest = [out_ref[...], up_ref[...], down_ref[...]]
    packed_ref[...] = jnp.concatenate([qkv_ref[0], qkv_ref[1], qkv_ref[2], *rest], 1)


def by_index_kernel(count, here_ref, *refs):
    blocks, outs = refs[:count], refs[count:]
    rows = blocks[0].shape[0]
    at = 0
    for ref in blocks:
        index = (here_ref[0] + at // rows) % RING
        start = pl.multiple_of(index * rows + at % rows, 16)
        at += ref.shape[0]
        left = 0
        for out_ref in outs:
            cols = out_ref.shape[1]
            out_ref[pl.ds(start, ref.shape[0]), :] = ref[:, left : left + cols]
            left += cols


def by_index(blocks, axis, cuts=None):
    rows, cols = blocks[0].shape
    vmem = pl.BlockSpec(memory_space=pltpu.VMEM)
    outs = [(RING * rows, n) for n in cuts or [cols]]
    found = pl.pallas_call(
        functools.partial(by_index_kernel, len(blocks)),
        out_shape=[jax.ShapeDtypeStruct(shape, BF16) for shape in outs],
        grid_spec=pltpu.PrefetchScalarGridSpec(
            num_scalar_prefetch=1,
            grid=(1,),
            in_specs=[vmem] * len(blocks),
            out_specs=[vmem] * len(outs),
        ),
        cost_estimate=cost(1),
        compiler_params=pltpu.CompilerParams(vmem_limit_bytes=16 * MIB),
    )(lax.axis_index(axis).astype(jnp.int32).reshape(1), *blocks)
    return found if cuts else found[0]


def head_lanes(width):
    lane = lax.broadcasted_iota(jnp.int32, (1, width), 1)
    return [(lane // HEAD_DIM) == h for h in range(width // HEAD_DIM)]


def heads_kernel(*refs):
    *blocks, out_ref = refs
    width = blocks[0].shape[1]
    count = out_ref.shape[0] // 2
    rows = count // 2 // RING
    for j, ref in enumerate([blocks[0], blocks[1], None, blocks[4]]):
        cols = slice(j * width, (j + 1) * width)
        if ref is None:
            ref = blocks[2]
            out_ref[count:, cols] = blocks[3][...]
        else:
            out_ref[count:, cols] = ref[count:]
        for at in range(0, count, count // 2):
            cut = (RING - j) * rows
            if j:
                out_ref[at : at + j * rows, cols] = ref[at + cut : at + count // 2]
            out_ref[at + j * rows : at + count // 2, cols] = ref[at : at + cut]


def two_sides(mine_ref, theirs_ref):
    width = mine_ref.shape[-1]
    return jnp.concatenate(
        [mine_ref[...].reshape(-1, width), theirs_ref[...].reshape(-1, width)], 0
    )


def head_scores(query, key, lanes, same_doc):
    query = jnp.where(lanes, query, jnp.zeros_like(query))
    return jnp.where(same_doc, dot(query, key, COL) * SCALE, -1e30)


def attend_kernel(mine_ref, theirs_ref, w_ref, bias_ref, id_col, id_row, qkv_ref, out_ref, log_ref):
    width = out_ref.shape[-1]
    projected = dot(two_sides(mine_ref, theirs_ref), w_ref[:, : 3 * width], ROW)
    qkv = (projected + bias_ref[...]).astype(BF16)
    qkv_ref[0] = qkv
    query, key, value = (qkv[:, i * width : (i + 1) * width] for i in range(3))
    same_doc = id_col[0] == id_row[0]
    out = jnp.zeros((qkv.shape[0], width), F32)
    for h, lanes in enumerate(head_lanes(width)):
        scores = head_scores(query, key, lanes, same_doc)
        top = jnp.max(scores, axis=1, keepdims=True)
        weight = jnp.exp(scores - top)
        total = jnp.sum(weight, axis=1, keepdims=True)
        log_ref[0, :, h : h + 1] = top + jnp.log(total)
        low = (weight * (1.0 / total)).astype(BF16)
        out = jnp.where(lanes, dot(low, value, ROW), out)
    out_ref[...] = out.astype(BF16).reshape(out_ref.shape)


def attend_back_kernel(
    mine_ref, theirs_ref, w_ref, qkv_ref, log_ref, id_col, id_row,
    d_ref, bias_ref, part_mine_ref, part_theirs_ref,
):
    width = d_ref.shape[-1] // 3
    d_heads = dot(two_sides(mine_ref, theirs_ref), w_ref[:, 3 * width :], ROW).astype(BF16)
    qkv = qkv_ref[0]
    query, key, value = (qkv[:, i * width : (i + 1) * width] for i in range(3))
    same_doc = id_col[0] == id_row[0]
    d_query = d_key = d_value = jnp.zeros((qkv.shape[0], width), F32)
    for h, lanes in enumerate(head_lanes(width)):
        scores = head_scores(query, key, lanes, same_doc)
        probs = jnp.exp(scores - log_ref[0, :, h : h + 1])
        d_prob = dot(jnp.where(lanes, d_heads, jnp.zeros_like(d_heads)), value, COL)
        row_dot = jnp.sum(probs * d_prob, axis=1, keepdims=True)
        d_score = (probs * (d_prob - row_dot)).astype(BF16)
        d_query = jnp.where(lanes, dot(d_score, key, ROW), d_query)
        d_key = jnp.where(lanes, dot(d_score, query, DOWN), d_key)
        d_value = jnp.where(lanes, dot(probs.astype(BF16), d_heads, DOWN), d_value)
    d_query, d_key = d_query * SCALE, d_key * SCALE
    d_all = jnp.concatenate([d_query, d_key, d_value], 1).astype(BF16)
    d_ref[...] = d_all.reshape(d_ref.shape)
    part = dot(d_all, w_ref[:, : 3 * width], COL).astype(BF16)
    half = part.shape[0] // 2
    part_mine_ref[...] = part[:half].reshape(part_mine_ref.shape)
    part_theirs_ref[...] = part[half:].reshape(part_theirs_ref.shape)
    bias_ref[0, 0:1] = jnp.sum(d_query, axis=0, keepdims=True)
    bias_ref[0, 1:2] = jnp.sum(d_value, axis=0, keepdims=True)


def ffn_kernel(
    hm_ref, ht_ref, wm_ref, wt_ref, x_ref, gain_ref, shift_ref, up_ref, down_ref, bias_ref,
    hidden_ref, act_ref, slope_ref, part_ref, resid_ref,
):
    for at in range(0, x_ref.shape[0], CHUNK):
        rows = slice(at, at + CHUNK)
        attended = dot(hm_ref[rows], wm_ref[...], COL) + dot(ht_ref[rows], wt_ref[...], COL)
        resid = x_ref[rows].astype(F32) + attended + shift_ref[0:1]
        if at == 0:
            resid_ref[...] = resid[: resid_ref.shape[0]]
        hidden = (normalise(resid)[0] * gain_ref[0:1] + shift_ref[1:2]).astype(BF16)
        hidden_ref[rows] = hidden
        pre_up = dot(hidden, up_ref[...], ROW) + bias_ref[...]
        cdf = 0.5 * (1.0 + lax.erf(pre_up * 0.5**0.5))
        activated = (pre_up * cdf).astype(BF16)
        act_ref[rows] = activated
        slope_ref[rows] = cdf + pre_up * jnp.exp(-0.5 * pre_up * pre_up) * 0.3989422804014327
        part_ref[rows] = dot(activated, down_ref[...], COL).astype(BF16)


def ffn_back_kernel(d_ffn_ref, slope_ref, up_ref, down_ref, d_ref, part_ref, sum_ref):
    sums = []
    for at in range(0, d_ffn_ref.shape[0], CHUNK):
        rows = slice(at, at + CHUNK)
        d_pre = dot(d_ffn_ref[rows], down_ref[...], ROW) * slope_ref[rows]
        low = d_pre.astype(BF16)
        d_ref[rows] = low
        part_ref[rows] = dot(low, up_ref[...], COL).astype(BF16)
        sums.append(jnp.sum(d_pre, axis=0, keepdims=True))
    sum_ref[...] = sum(sums)


def over_tokens(left_refs, right_refs):
    total, at = None, 0
    for i, ref in enumerate(left_refs):
        rows = ref.shape[0]
        right = right_refs[0][at : at + rows] if len(right_refs) == 1 else right_refs[i][...]
        term = dot(ref[...], right, DOWN)
        total, at = term if total is None else total + term, at + rows
    return total


def weight_grads_kernel(counts, n_in, here_ref, *refs):
    ins, outs = list(refs[:n_in]), refs[n_in:]
    first, second, right1, right2 = ([ins.pop(0) for _ in range(n)] for n in counts)
    rows = first[0].shape[1]
    low1 = over_tokens(first, right1).astype(BF16)
    low2 = over_tokens(second, right2).astype(BF16)
    values = jnp.concatenate([low1, low2], 1)
    if ins:
        small = ins[0][...]
        high = small.astype(BF16).astype(F32)
        packed = jnp.concatenate([high, small - high], 0).astype(BF16)
        values = jnp.concatenate([values, packed], 0)
    step = pl.program_id(0)
    if len(outs) == RING:
        places = [[(outs[i], 0, values.shape[0])] for i in range(RING)]
    else:
        half = rows // 2
        places = [[(outs[0], 0, rows)], [(outs[1], 0, rows)], [(outs[2], 0, half), (outs[3], half, rows)]]
        places.append([(outs[4], 0, rows)])
    for i in range(RING):

        @pl.when(step == i)
        def _(i=i):
            for out_ref, start, stop in places[i]:
                out_ref[...] = values[start:stop]


def weight_grads(first, second, right1, right2, small=None, mib=16):
    width = second[0].shape[1]
    rows = width // RING
    cols = right1[0].shape[1] + right2[0].shape[1]
    lefts = [*first, *second]
    counts = [len(v) for v in (first, second, right1, right2)]
    extra = 0 if small is None else 2 * small.shape[0]
    tail = [*right1, *right2] + ([] if small is None else [small])
    heights = [rows, rows, rows // 2, rows // 2, rows] if small is None else [rows + extra] * RING
    return pl.pallas_call(
        functools.partial(weight_grads_kernel, counts, len(lefts) + len(tail)),
        out_shape=[jax.ShapeDtypeStruct((n, cols), BF16) for n in heights],
        grid_spec=pltpu.PrefetchScalarGridSpec(
            num_scalar_prefetch=1,
            grid=(RING,),
            in_specs=[
                pl.BlockSpec((v.shape[0], rows), lambda i, here: (0, (here[0] + i) % RING))
                for v in lefts
            ]
            + [pl.BlockSpec(v.shape, lambda i, here: (0, 0)) for v in tail],
            out_specs=[pl.BlockSpec((n, cols), lambda i, here: (0, 0)) for n in heights],
        ),
        cost_estimate=cost(5),
        compiler_params=pltpu.CompilerParams(vmem_limit_bytes=mib * MIB),
    )(lax.axis_index("z").astype(jnp.int32).reshape(1), *lefts, *tail)


def sum_refs(refs, rows):
    return same_sum([ref[rows].astype(F32) for ref in refs])


def packed_sum(refs, first):
    values = sum_refs(refs, slice(first, None))
    count = values.shape[0] // 2
    return values[:count] + values[count:]


def relay_kernel(here_ref, *refs):
    attn, small, ffn, outs = refs[:4], refs[4:8], refs[8:11], refs[11:]
    low = sum_refs(attn, slice(None)).astype(BF16)
    values = packed_sum(small, 0)
    high = values.astype(BF16).astype(F32)
    packed = jnp.concatenate([high, values - high], 0).astype(BF16)
    own, right, left = (ref[...].astype(F32) for ref in ffn)
    grad = (own + (right + left)).astype(BF16)
    cols = low.shape[1]
    cuts = [grad[:, i : i + cols] for i in range(0, grad.shape[1], cols)]
    message = jnp.concatenate([low, *cuts, packed], 0)
    for i, out_ref in enumerate(outs):

        @pl.when(pl.program_id(0) == i)
        def _(out_ref=out_ref):
            out_ref[...] = message


def relay(attn, ffn, rows):
    cols, extra = attn[0].shape[1], attn[0].shape[0] - RING * rows
    wide = ffn[0].shape[1]
    height = rows * (1 + wide // cols) + extra

    def turned(n):
        return pl.BlockSpec((rows, n), lambda i, here: ((here[0] + i) % RING, 0))

    below = pl.BlockSpec((extra, cols), lambda i, here: (RING * rows // extra, 0))
    return pl.pallas_call(
        relay_kernel,
        out_shape=[jax.ShapeDtypeStruct((height, cols), BF16)] * RING,
        grid_spec=pltpu.PrefetchScalarGridSpec(
            num_scalar_prefetch=1,
            grid=(RING,),
            in_specs=[turned(cols)] * RING + [below] * RING + [turned(wide)] * 3,
            out_specs=[pl.BlockSpec((height, cols), lambda i, here: (0, 0))] * RING,
        ),
        cost_estimate=cost(2),
        compiler_params=pltpu.CompilerParams(vmem_limit_bytes=16 * MIB),
    )(lax.axis_index("x").astype(jnp.int32).reshape(1), *attn, *attn, *ffn)


def outputs_kernel(a_ref, b_ref, c_ref, d_ref, qkv, out, up, down, heads, units, gain, move):
    refs = (a_ref, b_ref, c_ref, d_ref)
    rows, width = qkv.shape[1:]
    values = sum_refs(refs, slice(0, rows))
    for i in range(3):
        qkv[i] = values[:, i * width : (i + 1) * width]
    out[...] = values[:, 3 * width :].T
    up[...] = sum_refs(refs, slice(rows, 2 * rows))
    down[...] = sum_refs(refs, slice(2 * rows, 3 * rows)).T
    small = packed_sum(refs, 3 * rows)
    cols, count = small.shape[1], gain.shape[0] + move.shape[0]
    pieces = gain.shape[1] // cols
    for i in range(pieces):
        span = slice(i * cols, (i + 1) * cols)
        gain[:, span] = small[i * count : i * count + gain.shape[0]]
        move[:, span] = small[i * count + gain.shape[0] : (i + 1) * count]
    units[...] = small[pieces * count : pieces * count + 1]
    last = small[pieces * count + 1 : pieces * count + 2]
    heads[0:1] = last[:, :width]
    heads[1:2] = last[:, width : 2 * width]


def total_of(refs):
    own, other, first, second, third = (ref[...].astype(F32) for ref in refs)
    return (own + other) + first + second + third


def rows_of(values):
    return jnp.concatenate([jnp.sum(v, axis=0, keepdims=True) for v in values], 0)


def second_norm_kernel(
    own_ref, other_ref, a_ref, b_ref, c_ref, resid1_ref, cot_ref, gain_ref, shift_ref,
    result_ref, d_ref, low_ref, sum_ref,
):
    normed = normalise(resid1_ref[...])[0] * gain_ref[0:1] + shift_ref[1:2]
    resid2 = normed + total_of((own_ref, other_ref, a_ref, b_ref, c_ref)) + shift_ref[2:3]
    unit, inverse = normalise(resid2)
    result_ref[...] = (unit * gain_ref[1:2] + shift_ref[3:4]).astype(BF16)
    cot = cot_ref[...].astype(F32)
    d_resid2 = normalise_back(cot * gain_ref[1:2], unit, inverse)
    d_ref[...] = d_resid2
    low_ref[...] = d_resid2.astype(BF16)
    sum_ref[...] = rows_of([cot * unit, d_resid2, cot])


def first_norm_kernel(
    own_ref, other_ref, a_ref, b_ref, c_ref, resid1_ref, d_resid2_ref, gain_ref, sum_ref, d_ref, sent_ref
):
    rows = d_ref.shape[0]
    d_normed = d_resid2_ref[...] + total_of((own_ref, other_ref, a_ref, b_ref, c_ref))
    unit, inverse = normalise(resid1_ref[...])
    d_resid1 = normalise_back(d_normed * gain_ref[0:1], unit, inverse)
    d_ref[...] = d_resid1
    sent_ref[0:rows] = d_resid1.astype(BF16)
    one = rows_of([d_normed * unit, d_resid1, d_normed])
    two = sum_ref[...]
    sums = jnp.concatenate([one[0:1], two[0:1], one[1:3], two[1:3]], 0)
    high = sums.astype(BF16)
    low = (sums - high.astype(F32)).astype(BF16)
    room = jnp.zeros((4, sums.shape[1]), F32)
    packed = jnp.concatenate([high.astype(F32), low.astype(F32), room], 0)
    sent_ref[rows : rows + 16] = packed.astype(BF16)


def on_device(
    tokens,
    segment_ids,
    qkv_weight,
    out_weight,
    up_weight,
    down_weight,
    head_bias,
    up_bias,
    gains,
    shifts,
    cotangent,
):
    seqs, rows, width = tokens.shape
    length = segment_ids.shape[1]
    count = seqs * length
    own = seqs * rows
    head_width = qkv_weight.shape[2]
    units = up_weight.shape[1]
    heads = head_width // HEAD_DIM
    y = lax.axis_index("y")
    core = lax.axis_index("core")

    vmem = pl.BlockSpec(memory_space=pltpu.VMEM)
    packed_width = 4 * head_width + 2 * units
    weights = call(
        1,
        weights_kernel,
        [((qkv_weight.shape[1], packed_width), BF16)],
        in_specs=[vmem] * 4,
        mib=60,
    )(qkv_weight, out_weight.T, up_weight, down_weight.T)[0]
    w_blocks = gather_direct(weights, "x")
    mine = tokens.reshape(own, width)
    one, three, *w_blocks = lax.optimization_barrier((shift(mine, "y", -1), shift(mine, "y", 1), *w_blocks))
    w_attn, w_ffn = by_index(w_blocks, "x", [4 * head_width, 2 * units])
    w_blocks = gather_direct(w_attn, "z")
    two = [shift(one[: own // 2], "y", -1), shift(three[own // 2 :], "y", 1)]
    *two, w_blocks[1], w_blocks[2], w_blocks[3] = lax.optimization_barrier((*two, *w_blocks[1:]))
    x_blocks = [mine, one, *two, three]
    w_attn = by_index(w_blocks, "z")

    ids = segment_ids.reshape(seqs, RING, 2, rows)
    ids = jnp.concatenate([ids, ids], 1)
    ids = lax.dynamic_slice_in_dim(ids, y, RING, 1)
    ids = jnp.where(core == 0, ids, ids[:, :, ::-1])
    ids = jnp.swapaxes(ids, 1, 2).reshape(seqs, length)
    ids = [ids[:, :, None], ids[:, None, :]]

    def by_seq(*block):
        return pl.BlockSpec(block, lambda s: tuple(s if n == 1 else 0 for n in block[:-2]) + (0, 0))

    def whole(*block):
        return pl.BlockSpec(block, lambda s: (0,) * len(block))

    side = by_seq(RING, 1, rows, width)
    id_specs = [
        pl.BlockSpec((1, length, 1), lambda s: (s, 0, 0)),
        pl.BlockSpec((1, 1, length), lambda s: (s, 0, 0)),
    ]

    def by_chip(sides):
        return [v.reshape(RING, seqs, rows, width) for v in sides]

    x_mine = assemble(x_blocks)
    x_sides = [x_mine, sibling(x_mine)]
    bias = jnp.concatenate([head_bias[0], jnp.zeros((head_width,), F32), head_bias[1]])
    qkv, head_out, log_total = call(
        4,
        attend_kernel,
        [
            ((seqs, length, 3 * head_width), BF16),
            ((2, RING, seqs, rows, head_width), BF16),
            ((seqs, length, heads), F32),
        ],
        (seqs,),
        [side, side, whole(width, 4 * head_width), whole(1, 3 * head_width)] + id_specs,
        [
            by_seq(1, length, 3 * head_width),
            by_seq(2, RING, 1, rows, head_width),
            by_seq(1, length, heads),
        ],
        mib=24,
    )(*by_chip(x_sides), w_attn, bias[None], *ids)
    head_out = head_out.reshape(count, head_width)
    w_ffn = after(w_ffn, head_out)
    heads_own = jnp.concatenate([head_out, w_attn[:, 3 * head_width :]], 0)
    one, three, w_one, w_three = lax.optimization_barrier(
        (shift(heads_own, "y", -1), shift(heads_own, "y", 1), shift(w_ffn, "z", -1), shift(w_ffn, "z", 1))
    )
    two = lax.optimization_barrier(
        (
            shift(one[: heads_own.shape[0] // 2], "y", -1),
            shift(three[heads_own.shape[0] // 2 :], "y", 1),
            shift(w_one[: w_ffn.shape[0] // 2], "z", -1),
            shift(w_three[w_ffn.shape[0] // 2 :], "z", 1),
        )
    )
    heads_blocks = [heads_own, one, two[0], two[1], three]
    w_ffn = by_index([w_ffn, w_one, two[2], two[3], w_three], "z")
    heads_mine = call(
        1.5,
        heads_kernel,
        [((count + width, 4 * head_width), BF16)],
        in_specs=[vmem] * 5,
    )(*heads_blocks)[0]
    heads_theirs = sibling(heads_mine)
    half = count // 2

    def rows_at(place, height, cols, left=0):
        return pl.BlockSpec((height, cols), lambda i: (place, left))

    w_specs = [rows_at(0, width, units), rows_at(0, width, units, 1)]
    ffn = []
    for which in (1, 0):
        ffn.append(
            call(
                4,
                ffn_kernel,
                [
                    ((half, width), BF16),
                    ((half, units), BF16),
                    ((half, units), F32),
                    ((half, width), BF16),
                    ((own, width), F32),
                ],
                (1,),
                [
                    rows_at(which, half, 4 * head_width),
                    rows_at(1 - which, half, 4 * head_width),
                    rows_at(1, width, 4 * head_width),
                    rows_at(1, width, 4 * head_width),
                    vmem,
                    vmem,
                    vmem,
                    *w_specs,
                    vmem,
                ],
                mib=32,
            )(
                heads_mine, heads_theirs, heads_mine, heads_theirs, x_sides[which], gains, shifts,
                w_ffn, w_ffn, up_bias[None],
            )
        )
    hidden, activated, slope, part, resid1 = zip(*ffn[::-1])
    resid1 = resid1[0]
    total, low = scatter_sides(*part)
    part_specs = [pl.BlockSpec((own, width), lambda i: (0, 0))] * 2
    result, d_resid2, d_resid2_low, second_sums = call(
        1.4,
        second_norm_kernel,
        [((own, width), BF16), ((own, width), F32), ((own, width), BF16), ((3, width), F32)],
        grid=(1,),
        in_specs=part_specs + [vmem] * 7,
    )(*total, *scatter_chips(low), resid1, cotangent.reshape(own, width), gains, shifts)

    d_ffn = gather_tokens(d_resid2_low)
    ffn = [
        call(
            1.7,
            ffn_back_kernel,
            [((half, units), BF16), ((half, width), BF16), ((1, units), F32)],
            (1,),
            [vmem, vmem, *w_specs],
            mib=24,
        )(d, s, w_ffn, w_ffn)
        for d, s in zip(d_ffn, slope)
    ]
    d_pre, part, unit_terms = zip(*ffn)
    unit_terms = unit_terms[0] + unit_terms[1]
    total, low = scatter_sides(*part)
    got = scatter_chips(low)
    grads = list(weight_grads(after_all(hidden, *low), d_ffn, d_pre, activated))
    d_resid1, sent = call(
        0.7,
        first_norm_kernel,
        [((own, width), F32), ((own + 16, width), BF16)],
        grid=(1,),
        in_specs=part_specs + [vmem] * 7,
    )(*total, *got, resid1, d_resid2, gains, second_sums)

    ring = ring_first(grads, "z")
    blocks = from_chips(after(sent, *ring))
    packed = pack(same_sum([unpack(b[own:], 6) for b in blocks]), 16)
    mine = assemble([b[:own] for b in blocks])
    d_attn = [mine, sibling(mine)]
    norm_terms = unpack(packed, 6) + unpack(sibling(packed), 6)
    d_proj, bias_terms, *part = call(
        8,
        attend_back_kernel,
        [
            ((2, RING, seqs, rows, 3 * head_width), BF16),
            ((seqs, 2, head_width), F32),
            ((RING, seqs, rows, width), BF16),
            ((RING, seqs, rows, width), BF16),
        ],
        (seqs,),
        [side, side, whole(width, 4 * head_width)]
        + [by_seq(1, length, 3 * head_width), by_seq(1, length, heads)]
        + id_specs,
        [by_seq(2, RING, 1, rows, 3 * head_width), by_seq(1, 2, head_width), side, side],
        mib=32,
    )(*by_chip(d_attn), w_attn, qkv, log_total, *ids)
    grads = ring_second(grads, ring, "z")
    d_proj = d_proj.reshape(count, 3 * head_width)
    bias_terms = jnp.sum(bias_terms, 0)
    cols = 4 * head_width
    pieces = [norm_terms[:, i : i + cols] for i in range(0, width, cols)]
    pieces += [unit_terms.reshape(-1, cols), bias_terms.reshape(1, 2 * head_width)]
    pieces[-1] = jnp.pad(pieces[-1], ((0, 0), (0, cols - 2 * head_width)))
    small = jnp.concatenate(pieces, 0)
    small = jnp.pad(small, ((0, -small.shape[0] % 8), (0, 0)))
    messages = weight_grads(x_sides, d_attn, [d_proj], [head_out], small, 60)
    messages = exchange(messages, "z")
    total, low = scatter_sides(*(p.reshape(half, width) for p in part))
    got = scatter_chips(low)
    grad_tokens = d_resid1 + total[0][:own].astype(F32) + total[1][:own].astype(F32)
    grad_tokens = grad_tokens + got[0].astype(F32) + got[1].astype(F32) + got[2].astype(F32)
    messages[3] = after(messages[3], got[0])
    messages = exchange(relay(messages, grads, rows), "x")
    weights_out = list(call(
        2,
        outputs_kernel,
        [
            ((3, rows, head_width), F32),
            ((head_width, rows), F32),
            ((rows, units), F32),
            ((units, rows), F32),
            ((2, head_width), F32),
            ((1, units), F32),
            ((2, width), F32),
            ((4, width), F32),
        ],
        in_specs=[vmem] * 4,
    )(*messages))
    weights_out[5] = weights_out[5].reshape(units)
    return (result.reshape(tokens.shape), grad_tokens.reshape(tokens.shape), *weights_out)


def solution(mesh):
    mesh = Mesh(mesh.devices.reshape(RING, RING, RING, 2), ("z", "x", "y", "core"))
    dp, mp = ("z", "x"), ("y", "core")
    in_specs = (
        P(dp, mp, None),
        P(dp, None),
        P(None, dp, mp),
        P(mp, dp),
        P(dp, mp),
        P(mp, dp),
        P(None, mp),
        P(mp),
        P(),
        P(),
        P(dp, mp, None),
    )
    out_specs = (
        P(dp, mp, None),
        P(dp, mp, None),
        P(None, dp, mp),
        P(mp, dp),
        P(dp, mp),
        P(mp, dp),
        P(None, mp),
        P(mp),
        P(),
        P(),
    )
    return jax.shard_map(
        on_device, mesh=mesh, in_specs=in_specs, out_specs=out_specs, check_vma=False
    )
```
